128 devices in a mesh: member: 16 (over y_lo, x, core), fsdp: 8 (over y_hi, z).
Axes of the slice: x: 4, y: 4 (y_hi: 2, y_lo: 2; y = y_hi * 2 + y_lo), z: 4, core: 2. Of those that a mesh axis runs over, the one named last changes fastest.
Arguments:
- tokens: bfloat16 [16, 1024, 1536], P('member', 'fsdp'), may hold values from -48 to 48
- upstream: bfloat16 [16, 1024, 1536], P('member', 'fsdp'), may hold values from -6 to 6
- gate_weight: bfloat16 [16, 1536, 6144], P('member', None, 'fsdp'), may hold values from -0.15625 to 0.15625
- up_weight: bfloat16 [16, 1536, 6144], P('member', None, 'fsdp'), may hold values from -0.15625 to 0.15625
- down_weight: bfloat16 [16, 6144, 1536], P('member', 'fsdp'), may hold values from -0.078125 to 0.078125
- norm_gain: bfloat16 [16, 1536], P('member'), may hold values from 0.099609375 to 1.8984375
- stale_gate: bfloat16 [16, 1536, 6144], P('member', None, 'fsdp'), may hold values from -0.15625 to 0.15625
- stale_up: bfloat16 [16, 1536, 6144], P('member', None, 'fsdp'), may hold values from -0.15625 to 0.15625
- stale_down: bfloat16 [16, 6144, 1536], P('member', 'fsdp'), may hold values from -0.078125 to 0.078125
- stale_gain: bfloat16 [16, 1536], P('member'), may hold values from 0.099609375 to 1.8984375
Outputs:
- grad_tokens: bfloat16 [16, 1024, 1536], P('member', 'fsdp')
- grad_gate: bfloat16 [16, 1536, 6144], P('member', None, 'fsdp')
- grad_up: bfloat16 [16, 1536, 6144], P('member', None, 'fsdp')
- grad_down: bfloat16 [16, 6144, 1536], P('member', 'fsdp')
- grad_gain: float32 [16, 1536], P('member')
The draws below stay inside these ranges and needn't reach their ends.
All inputs are finite; a program needn't handle non-finite values.
Results may differ from the reference program's by a relative error of at most 0.02.
Values may be sent and summed in bfloat16 or wider, within the bound.
A program may use at most 128 MiB of HBM per device.

```python
import math
import jax
import jax.numpy as jnp
from jax import lax

D = 1536
FF = 6144
MEMBERS = 16
TOKENS = 1024
N_FSDP = 8


def draw_tokens(key, part):
    key = jax.random.fold_in(key, 11)
    first_key, second_key, third_key = jax.random.split(key, 3)
    entries = jnp.clip(jax.random.normal(first_key, (MEMBERS, TOKENS, D), jnp.float32), -4.0, 4.0)
    row_scale = jnp.exp(jax.random.uniform(second_key, (MEMBERS, TOKENS, 1), jnp.float32, math.log(0.3), math.log(3.0)))
    column_scale = jnp.exp(jax.random.uniform(third_key, (MEMBERS, 1, D), jnp.float32, math.log(0.4), math.log(4.0)))
    return (entries * row_scale * column_scale).astype(jnp.bfloat16)


def shard_levels(own_key, shape, cuts, least, top_value):
    level, own = 1.0, jax.random.fold_in(own_key, 6)
    for position, shards_of in cuts:
        heights = jnp.exp(jax.random.uniform(jax.random.fold_in(own, position), (shards_of,), jnp.float32, least / len(cuts), top_value / len(cuts)))
        level = level * jnp.repeat(heights, shape[position] // shards_of).reshape([-1 if axis == position else 1 for axis in range(len(shape))])
    return level


def scatter_about(rng, dims, spread, bound, shards=(), dtype=jnp.bfloat16):
    factor_of = shard_levels(rng, dims, shards, -0.22, 0.18) if shards else 1.0
    result = jax.random.normal(rng, dims, jnp.float32) * spread * factor_of
    return jnp.minimum(jnp.maximum(result, -bound), bound).astype(dtype)


def setup_inputs(seed: int = 0) -> dict:
    key_list = jax.random.split(jax.random.key(seed), 11)
    tokens = draw_tokens(jax.random.fold_in(key_list[10], 71), 0)
    upstream = scatter_about(key_list[1], (MEMBERS, TOKENS, D), 1.0, 6.0, ((0, 16), (1, 8)))
    gate_weight = scatter_about(key_list[2], (MEMBERS, D, FF), D ** -0.5, 0.15625, ((0, 16), (2, 8)))
    up_weight = scatter_about(key_list[3], (MEMBERS, D, FF), D ** -0.5, 0.15625, ((0, 16), (2, 8)))
    down_weight = scatter_about(key_list[4], (MEMBERS, FF, D), FF ** -0.5, 0.078125, ((0, 16), (1, 8)))
    norm_gain = jnp.clip(1.0 + 0.18 * jax.random.normal(key_list[5], (MEMBERS, D), jnp.float32), 0.099609375, 1.8984375).astype(jnp.bfloat16)
    stale_gate = scatter_about(key_list[6], (MEMBERS, D, FF), D ** -0.5, 0.15625, ((0, 16), (2, 8)))
    stale_up = scatter_about(key_list[7], (MEMBERS, D, FF), D ** -0.5, 0.15625, ((0, 16), (2, 8)))
    stale_down = scatter_about(key_list[8], (MEMBERS, FF, D), FF ** -0.5, 0.078125, ((0, 16), (1, 8)))
    stale_gain = jnp.clip(1.0 + 0.18 * jax.random.normal(key_list[9], (MEMBERS, D), jnp.float32), 0.099609375, 1.8984375).astype(jnp.bfloat16)
    return {"tokens": tokens, "upstream": upstream, "gate_weight": gate_weight, "up_weight": up_weight, "down_weight": down_weight, "norm_gain": norm_gain, "stale_gate": stale_gate, "stale_up": stale_up, "stale_down": stale_down, "stale_gain": stale_gain}


EPS = 1e-05
AGREE = 1.0

def normalize(rows_in):
    values = rows_in.astype(jnp.float32)
    inverse = lax.rsqrt(lax.optimization_barrier(jnp.mean(values * values, axis=-1, keepdims=True)) + EPS)
    return (values * inverse, inverse)

def project_up(inputs, gate_weight, up_weight):
    gate_value = jnp.dot(inputs, gate_weight, preferred_element_type=jnp.float32)
    up_value = jnp.dot(inputs, up_weight, preferred_element_type=jnp.float32)
    hidden = (jax.nn.silu(gate_value) * up_value).astype(jnp.bfloat16)
    return (gate_value, up_value, hidden)

def blocked_sum(pairs):
    total = None
    for left, right in pairs:
        row_total = left.shape[0]
        width = right.shape[0] // N_FSDP
        left_blocks = left.reshape(row_total, N_FSDP, width).transpose(1, 0, 2).astype(jnp.float32)
        right_blocks = right.reshape(N_FSDP, width, right.shape[1]).astype(jnp.float32)
        term = jnp.einsum('krf,kfd->krd', left_blocks, right_blocks)
        total = term if total is None else total + term
    rounded = lax.optimization_barrier(total.astype(jnp.bfloat16))
    return lax.optimization_barrier(jnp.sum(rounded.astype(jnp.float32), axis=0))

def one_member(arrays):
    tokens, upstream, gate_weight, up_weight, down_weight, norm_gain, peer_gate, peer_up, peer_down, peer_gain = arrays
    normed, inverse = normalize(tokens)
    gain_value = norm_gain.astype(jnp.float32)
    inputs = (normed * gain_value).astype(jnp.bfloat16)
    peer_inputs = (normed * peer_gain.astype(jnp.float32)).astype(jnp.bfloat16)
    gate_value, up_value, hidden = project_up(inputs, gate_weight, up_weight)
    peer_hidden = project_up(peer_inputs, peer_gate, peer_up)[2]
    out_gap = blocked_sum(((hidden, down_weight), (peer_hidden, -peer_down)))
    grad_out = (upstream.astype(jnp.float32) + AGREE * out_gap).astype(jnp.bfloat16)
    grad_hidden = jnp.dot(grad_out, down_weight.T, preferred_element_type=jnp.float32)
    sigma = jax.nn.sigmoid(gate_value)
    grad_gate_pre = (grad_hidden * up_value * sigma * (1.0 + gate_value * (1.0 - sigma))).astype(jnp.bfloat16)
    grad_up_pre = (grad_hidden * jax.nn.silu(gate_value)).astype(jnp.bfloat16)
    grad_down = jnp.dot(hidden.T, grad_out, preferred_element_type=jnp.float32).astype(jnp.bfloat16)
    grad_gate = jnp.dot(inputs.T, grad_gate_pre, preferred_element_type=jnp.float32).astype(jnp.bfloat16)
    grad_up = jnp.dot(inputs.T, grad_up_pre, preferred_element_type=jnp.float32).astype(jnp.bfloat16)
    grad_inputs = blocked_sum(((grad_gate_pre, gate_weight.T), (grad_up_pre, up_weight.T)))
    grad_gain = lax.optimization_barrier(jnp.sum(grad_inputs * normed, axis=0))
    grad_normed = grad_inputs * gain_value
    grad_tokens = grad_out.astype(jnp.float32) + inverse * (grad_normed - normed * lax.optimization_barrier(jnp.mean(grad_normed * normed, axis=-1, keepdims=True)))
    return (grad_tokens.astype(jnp.bfloat16), grad_gate, grad_up, grad_down, grad_gain)

def reference(tokens, upstream, gate_weight, up_weight, down_weight, norm_gain, stale_gate, stale_up, stale_down, stale_gain):
    peer_gate = jnp.roll(stale_gate, 1, axis=0)
    peer_up = jnp.roll(stale_up, 1, axis=0)
    peer_down = jnp.roll(stale_down, 1, axis=0)
    peer_gain = jnp.roll(stale_gain, 1, axis=0)
    results = lax.map(one_member, (tokens, upstream, gate_weight, up_weight, down_weight, norm_gain, peer_gate, peer_up, peer_down, peer_gain))
    return (results[0], results[1], results[2], results[3], results[4])
```

```python
import functools
import jax
import jax.numpy as jnp
from jax import lax
from jax.experimental import pallas as pl
from jax.experimental.pallas import tpu as pltpu
from jax.sharding import PartitionSpec as P

EPS = 1e-05
AGREE = 1.0
MESH = pl.DeviceIdType.MESH
F32 = jnp.float32
BF16 = jnp.bfloat16
D = 1536
FB = 768
N = 8
ROWS = 128
NB = 4
RB = ROWS // NB
M = N * RB

ORDER = (
    ("E1", 0), ("E2", 0), ("E3", 0), ("E5", 0), ("E1", 1), ("E4", 0), ("E3", 1), ("E6", 0), ("E5", 1),
    ("E2", 1), ("E7", 0), ("E1", 2), ("O1", 0), ("O2", 0), ("E4", 1), ("E6", 1), ("O3", 0), ("E3", 2),
    ("E5", 2), ("P1", 0), ("E7", 1), ("E2", 2), ("E1", 3), ("P2", 0), ("P3", 0), ("E4", 2), ("E6", 2),
    ("P4", 0), ("E3", 3), ("E5", 3), ("O1", 1), ("O2", 1), ("E7", 2), ("E2", 3), ("P1", 1), ("P2", 1),
    ("E4", 3), ("E6", 3), ("P3", 1), ("P4", 1), ("O3", 1), ("E7", 3), ("O1", 2), ("O2", 2), ("F0", 0),
    ("P1", 2), ("P2", 2), ("P3", 2), ("F2", 0), ("F2b", 0), ("P4", 2), ("P1", 3), ("P2", 3), ("F0", 1),
    ("F3", 0), ("P3", 3), ("P4", 3), ("O3", 2), ("F4", 0), ("F2", 1), ("F2b", 1), ("O1", 3), ("O2", 3),
    ("F0", 2), ("G2", 0), ("G3", 0), ("G5", 0), ("O3", 3), ("F3", 1), ("F2", 2), ("F2b", 2), ("F4", 1),
    ("F0", 3), ("G4", 0), ("G3", 1), ("G6", 0), ("F3", 2), ("G5", 1), ("F2b", 3), ("G2", 1), ("F4", 2),
    ("F2", 3), ("G7", 0), ("B1", 0), ("G3", 2), ("B2", 0), ("G4", 1), ("G6", 1), ("B3", 0), ("B4", 0),
    ("G2", 2), ("G5", 2), ("F3", 3), ("G4", 2), ("G6", 2), ("G7", 1), ("B1", 1), ("F4", 3), ("S2", 0),
    ("S2b", 0), ("B2", 1), ("B3", 1), ("B4", 1), ("G3", 3), ("G7", 2), ("B1", 2), ("B2", 2), ("G2", 3),
    ("G5", 3), ("B3", 2), ("S3", 0), ("B4", 2), ("S2", 1), ("S2b", 1), ("S4", 0), ("G4", 3), ("G6", 3),
    ("S2b", 2), ("S2", 2), ("S3", 1), ("G7", 3), ("B1", 3), ("S3", 2), ("B2", 3), ("S4", 1), ("B3", 3),
    ("B4", 3), ("S4", 2), ("K1", 0), ("WD", 0), ("WD", 1), ("S2", 3), ("S2b", 3), ("K2", 0), ("WD", 2),
    ("WG", 0), ("WG", 1), ("WG", 2), ("WG", 3), ("S3", 3), ("WG", 4), ("WG", 5), ("WU", 0), ("WU", 1),
    ("WU", 2), ("WU", 3), ("S4", 3), ("WU", 4), ("WU", 5),
)


def dot_nn(a, b):
    return jnp.dot(a, b, preferred_element_type=F32)


def dot_nt(a, b):
    return lax.dot_general(a, b, (((1,), (1,)), ((), ())), preferred_element_type=F32)


def dot_tn(a, b):
    return lax.dot_general(a, b, (((0,), (0,)), ((), ())), preferred_element_type=F32)


def blocks(total, size, body):
    @pl.loop(0, total // size)
    def _(i):
        body(pl.multiple_of(i * size, size))


def kernel(
    tokens, upstream, gate_w, up_w, down_w, gain, stale_gate, stale_up, stale_down, stale_gain,
    out_tokens, out_gate, out_up, out_down, out_gain,
    wg, wu, wd, sg, su, sd, ups, tok, tok_next, x, xs, inv, gv, uv, gt, ut, hid, hid_s,
    gap, peer, rs1, rs2, go, ggp, gup, outt, acc, acc_in, gain_buf,
    send, recv, local,
):
    member = lax.axis_index("member")
    j = lax.axis_index("fsdp")
    y, z = j // 4, j % 4
    members = lax.axis_size("member")
    z_up, z_dn, z_far = (z + 1) % 4, (z + 3) % 4, (z + 2) % 4
    other = 1 - y
    UP, DN, ACROSS = (member, y * 4 + z_up), (member, y * 4 + z_dn), (member, other * 4 + z)
    NEXT = ((member + 1) % members, j)
    PREV = ((member + members - 1) % members, j)

    pos = {
        "o": j,
        "ou": y * 4 + z_up,
        "od": y * 4 + z_dn,
        "of": y * 4 + z_far,
        "x": other * 4 + z,
        "xu": other * 4 + z_up,
        "xd": other * 4 + z_dn,
        "xf": other * 4 + z_far,
    }

    def rows(b, chunk):
        return pl.ds(pl.multiple_of(b * M + pos[chunk] * RB, 16), RB)

    def batch(b):
        return pl.ds(b * M, M)

    numbers = {}

    def number(key):
        return numbers.setdefault(key, len(numbers))

    def remote(key, src, dst, device):
        i = number(key)
        return pltpu.make_async_remote_copy(
            src_ref=src,
            dst_ref=dst,
            send_sem=send.at[i],
            recv_sem=recv.at[i],
            device_id=device,
            device_id_type=MESH,
        )

    sent = []

    def start(key, src, dst, device):
        copy = remote(key, src, dst, device)
        copy.start()
        sent.append((key, copy))

    def arrive(key, dst, device):
        remote(key, dst, dst, device).wait_recv()

    locals_ = {}

    def fetch(key, src, dst):
        copy = pltpu.make_async_copy(src, dst, local.at[len(locals_)])
        locals_[key] = copy
        copy.start()

    done = set()

    def need(key):
        if key not in done:
            done.add(key)
            locals_[key].wait()

    for b in range(NB):
        fetch(("t", b), tokens.at[0, pl.ds(b * RB, RB)], tok.at[rows(b, "o")])
    fetch("sg", stale_gate.at[0], sg)
    fetch("su", stale_up.at[0], su)
    fetch("sd", stale_down.at[0], sd)
    fetch("wg", gate_w.at[0], wg)
    fetch("wu", up_w.at[0], wu)
    fetch("wd", down_w.at[0], wd)
    fetch("ups", upstream.at[0], ups)

    barrier = pltpu.get_barrier_semaphore()
    for step in range(1, N):
        pl.semaphore_signal(barrier, inc=1, device_id=(member, (j + step) % N), device_id_type=MESH)
    for device in (NEXT, PREV):
        pl.semaphore_signal(barrier, inc=1, device_id=device, device_id_type=MESH)
    pl.semaphore_wait(barrier, N + 1)
    acc[...] = jnp.zeros_like(acc)

    def onward(b, chunk):
        start(("n", b, chunk), tok.at[rows(b, chunk)], tok_next.at[rows(b, chunk)], PREV)

    def gather(name, ref, then):
        def move(b, chunk, way, device):
            start((name, b, chunk, way), ref.at[rows(b, chunk)], ref.at[rows(b, chunk)], device)

        def got(b, chunk, sent_as, way):
            arrive((name, b, sent_as, way), ref.at[rows(b, chunk)], UP)
            then(b, chunk)

        def e1(b):
            if name == "a":
                need(("t", b))
            for way, device in (("u", UP), ("a", ACROSS), ("d", DN)):
                move(b, "o", way, device)
            then(b, "o")

        def e2(b):
            got(b, "od", "o", "u")
            move(b, "od", "u", UP)

        def e3(b):
            got(b, "x", "o", "a")
            move(b, "x", "d", DN)
            move(b, "x", "u", UP)

        def e4(b):
            got(b, "xu", "x", "d")
            move(b, "xu", "d", DN)

        def e5(b):
            got(b, "ou", "o", "d")

        def e6(b):
            got(b, "xd", "x", "u")

        def e7(b):
            got(b, "of", "od", "u")
            got(b, "xf", "xu", "d")

        return e1, e2, e3, e4, e5, e6, e7

    def scatter(name, ref, land, first_key):
        def slot(b, k):
            return land.at[pl.ds((b * 7 + k) * RB, RB)]

        def push(b, chunk, k, device):
            start((name, b, k), ref.at[rows(b, chunk)], slot(b, k), device)

        def landed(b, k):
            arrive((name, b, k), slot(b, k), UP)

        def add(b, chunk, slots):
            r = rows(b, chunk)
            total = ref[r, :].astype(F32)
            for k in slots:
                total = total + slot(b, k)[...].astype(F32)
            return r, total

        def f1(b):
            push(b, "xf", 0, UP)
            push(b, "of", 1, DN)
            push(b, "xd", 3, DN)
            push(b, "ou", 2, UP)

        def f2(b):
            landed(b, 0)
            r, total = add(b, "xu", (0,))
            ref[r, :] = total.astype(BF16)
            push(b, "xu", 4, UP)

        def f2b(b):
            landed(b, 1)
            r, total = add(b, "od", (1,))
            ref[r, :] = total.astype(BF16)
            push(b, "od", 5, DN)

        def f3(b):
            landed(b, 3)
            landed(b, 4)
            r, total = add(b, "x", (3, 4))
            ref[r, :] = total.astype(BF16)
            push(b, "x", 6, ACROSS)

        def f4(b):
            for k in (2, 5, 6):
                landed(b, k)

        def result(b, first, size):
            at = pl.multiple_of(b * M + j * RB + first, 16)
            total = ref[pl.ds(at, size), :].astype(F32)
            for k in (2, 5, 6):
                total = total + land[pl.ds((b * 7 + k) * RB + first, size), :].astype(F32)
            return total

        return f1, f2, f2b, f3, f4, result

    ea = gather("a", tok, onward)
    eg = gather("g", go, lambda b, chunk: None)
    ra = scatter("r", gap, rs1, None)
    rg = scatter("s", peer, rs2, None)

    gain_row = gain[...].astype(F32)
    stale_row = stale_gain[...].astype(F32)

    def normalize(src, dst, at_dst, b, factor, keep):
        def body(at):
            values = src[pl.ds(pl.multiple_of(b * M + at, 16), 16), :].astype(F32)
            scale = lax.rsqrt(jnp.mean(values * values, axis=-1, keepdims=True) + EPS)
            dst[pl.ds(pl.multiple_of(at_dst + at, 16), 16), :] = (values * scale * factor).astype(BF16)
            if keep:
                inv[pl.ds(pl.multiple_of(b * M + at, 16), 16), :] = scale

        blocks(M, 16, body)

    def activate(g_ref, u_ref, base, dst, at_dst):
        def body(at):
            g = g_ref[pl.ds(pl.multiple_of(base + at, 16), 16), :]
            u = u_ref[pl.ds(pl.multiple_of(base + at, 16), 16), :]
            dst[pl.ds(pl.multiple_of(at_dst + at, 16), 16), :] = (g * jax.nn.sigmoid(g) * u).astype(BF16)

        blocks(M, 16, body)

    def p1(b):
        for chunk in pos:
            arrive(("n", b, chunk), tok_next.at[rows(b, chunk)], PREV)
        normalize(tok_next, xs, 0, b, stale_row, False)

    def p2(b):
        need("sg")
        gt[...] = dot_nn(xs[...], sg[...])

    def p3(b):
        need("su")
        ut[...] = dot_nn(xs[...], su[...])
        activate(gt, ut, 0, hid_s, 0)

    def p4(b):
        need("sd")
        peer[batch(b), :] = dot_nn(hid_s[...], sd[...]).astype(BF16)
        start(("p", b), peer.at[batch(b)], gap.at[batch(b)], NEXT)

    def o1(b):
        normalize(tok, x, b * M, b, gain_row, True)

    def o2(b):
        need("wg")
        gv[batch(b), :] = dot_nn(x[batch(b), :], wg[...])

    def o3(b):
        need("wu")
        uv[batch(b), :] = dot_nn(x[batch(b), :], wu[...])
        activate(gv, uv, b * M, hid, b * M)

    def f0(b):
        need("wd")
        arrive(("p", b), gap.at[batch(b)], PREV)
        own = dot_nn(hid[batch(b), :], wd[...])
        gap[batch(b), :] = (own - gap[batch(b), :].astype(F32)).astype(BF16)
        ra[0](b)

    def f4(b):
        need("ups")
        ra[4](b)
        for first in range(0, RB, 16):
            total = ra[5](b, first, 16)
            mine = ups[pl.ds(b * RB + first, 16), :].astype(F32) + AGREE * total
            go[pl.ds(pl.multiple_of(b * M + j * RB + first, 16), 16), :] = mine.astype(BF16)
        eg[0](b)

    def b1(b):
        gt[...] = dot_nt(go[batch(b), :], wd[...])

        def body(at):
            g = gv[pl.ds(pl.multiple_of(b * M + at, 16), 16), :]
            s = jax.nn.sigmoid(g)
            gh = gt[pl.ds(at, 16), :]
            u = uv[pl.ds(pl.multiple_of(b * M + at, 16), 16), :]
            ggp[pl.ds(pl.multiple_of(b * M + at, 16), 16), :] = (gh * u * s * (1.0 + g * (1.0 - s))).astype(BF16)
            gup[pl.ds(pl.multiple_of(b * M + at, 16), 16), :] = (gh * (g * s)).astype(BF16)

        blocks(M, 16, body)

    def back(b, half):
        if half == 0:
            for key, copy in sent:
                if key == ("p", b):
                    copy.wait_send()
            waited.add(("p", b))
        cols = pl.ds(half * FB, FB)
        total = dot_nt(ggp[batch(b), :], wg[cols, :]) + dot_nt(gup[batch(b), :], wu[cols, :])
        peer[batch(b), cols] = total.astype(BF16)

    waited = set()

    def b2(b):
        back(b, 0)

    def b3(b):
        back(b, 1)
        rg[0](b)

    def b4(b):
        def body(at):
            r = pl.ds(pl.multiple_of(b * M + at, 16), 16)
            part = part_of[r, :].astype(F32) * (tok[r, :].astype(F32) * inv[r, :])
            acc[...] += part[:8] + part[8:]

        part_of = peer
        blocks(M, 16, body)

    def k1(b):
        for step in range(1, N):
            start(("k", step), acc, acc_in.at[step], (member, (j + step) % N))

    def k2(b):
        total = acc[...]
        for step in range(1, N):
            arrive(("k", step), acc_in.at[step], (member, (j + step) % N))
            total = total + acc_in[step]
        gain_buf[...] = jnp.sum(total, axis=0, keepdims=True)
        fetch("ok", gain_buf, out_gain)

    def f4g(b):
        rg[4](b)
        for first in range(0, RB, 16):
            grad_in = rg[5](b, first, 16)
            r = pl.ds(pl.multiple_of(b * M + j * RB + first, 16), 16)
            scale = inv[r, :]
            normed = tok[r, :].astype(F32) * scale
            grad_normed = grad_in * gain_row
            mean = jnp.mean(grad_normed * normed, axis=-1, keepdims=True)
            outt[pl.ds(b * RB + first, 16), :] = (
                go[r, :].astype(F32) + scale * (grad_normed - normed * mean)
            ).astype(BF16)
        fetch(("ot", b), outt.at[pl.ds(b * RB, RB)], out_tokens.at[0, pl.ds(b * RB, RB)])

    def weight(name, left, right, dst, out, size):
        def task(i):
            r = pl.ds(i * size, size)
            dst[r, :] = dot_tn(left[:, i * size : (i + 1) * size], right[...]).astype(BF16)
            fetch((name, i), dst.at[r], out.at[0, r])

        return task

    tasks = {
        "P1": p1, "P2": p2, "P3": p3, "P4": p4, "O1": o1, "O2": o2, "O3": o3, "F0": f0, "F4": f4,
        "F2": ra[1], "F2b": ra[2], "F3": ra[3], "S2": rg[1], "S2b": rg[2], "S3": rg[3], "S4": f4g,
        "B1": b1, "B2": b2, "B3": b3, "B4": b4, "K1": k1, "K2": k2,
        "WD": weight("wd", hid, go, sd, out_down, 256),
        "WG": weight("wg", x, ggp, sg, out_gate, 256),
        "WU": weight("wu", x, gup, su, out_up, 256),
    }
    for i in range(7):
        tasks["E%d" % (i + 1)] = ea[i]
        tasks["G%d" % (i + 1)] = eg[i]
    for name, index in ORDER:
        tasks[name](index)

    for key, copy in sent:
        if key not in waited:
            copy.wait_send()
    for key in locals_:
        need(key)


def shards(
    tokens, upstream, gate_weight, up_weight, down_weight, norm_gain,
    stale_gate, stale_up, stale_down, stale_gain,
):
    hbm = pl.BlockSpec(memory_space=pl.ANY)
    vmem = pl.BlockSpec(memory_space=pltpu.VMEM)
    total = N * ROWS
    wide = pltpu.VMEM((total, D), BF16)
    narrow = pltpu.VMEM((total, FB), F32)
    half = pltpu.VMEM((total, FB), BF16)
    tall = pltpu.VMEM((D, FB), BF16)
    flat = pltpu.VMEM((FB, D), BF16)
    step = pltpu.VMEM((M, FB), F32)
    land = pltpu.VMEM((NB * 7 * RB, D), BF16)
    return pl.pallas_call(
        kernel,
        out_shape=(
            jax.ShapeDtypeStruct((1, ROWS, D), BF16),
            jax.ShapeDtypeStruct((1, D, FB), BF16),
            jax.ShapeDtypeStruct((1, D, FB), BF16),
            jax.ShapeDtypeStruct((1, FB, D), BF16),
            jax.ShapeDtypeStruct((1, D), F32),
        ),
        in_specs=[hbm, hbm, hbm, hbm, hbm, vmem, hbm, hbm, hbm, vmem],
        out_specs=(hbm,) * 5,
        scratch_shapes=[
            tall, tall, flat, tall, tall, flat,
            pltpu.VMEM((ROWS, D), BF16),
            wide, wide, wide,
            pltpu.VMEM((M, D), BF16),
            pltpu.VMEM((total, 1), F32),
            narrow, narrow, step, step, half,
            pltpu.VMEM((M, FB), BF16),
            wide, wide, land, land, wide, half, half,
            pltpu.VMEM((ROWS, D), BF16),
            pltpu.VMEM((8, D), F32),
            pltpu.VMEM((N, 8, D), F32),
            pltpu.VMEM((1, D), F32),
            pltpu.SemaphoreType.DMA((NB * 37 + 8,)),
            pltpu.SemaphoreType.DMA((NB * 37 + 8,)),
            pltpu.SemaphoreType.DMA((2 * NB + 7 + 16,)),
        ],
        compiler_params=pltpu.CompilerParams(
            collective_id=0, has_side_effects=True, vmem_limit_bytes=62 * 2**20
        ),
        name="layer",
    )(
        tokens, upstream, gate_weight, up_weight, down_weight, norm_gain,
        stale_gate, stale_up, stale_down, stale_gain,
    )


def solution(mesh):
    in_specs = (
        P("member", "fsdp", None),
        P("member", "fsdp", None),
        P("member", None, "fsdp"),
        P("member", None, "fsdp"),
        P("member", "fsdp", None),
        P("member", None),
        P("member", None, "fsdp"),
        P("member", None, "fsdp"),
        P("member", "fsdp", None),
        P("member", None),
    )
    out_specs = (
        P("member", "fsdp", None),
        P("member", None, "fsdp"),
        P("member", None, "fsdp"),
        P("member", "fsdp", None),
        P("member", None),
    )
    return jax.shard_map(shards, mesh=mesh, in_specs=in_specs, out_specs=out_specs, check_vma=False)
```

```python
import functools
import jax
import jax.numpy as jnp
from jax import lax
from jax.experimental import pallas as pl
from jax.experimental.pallas import tpu as pltpu
from jax.sharding import PartitionSpec as P

EPS = 1e-05
AGREE = 1.0
MESH = pl.DeviceIdType.MESH
F32 = jnp.float32
BF16 = jnp.bfloat16
D = 1536
FB = 768
N = 8
ROWS = 128
NB = 4
RB = ROWS // NB
M = N * RB

ORDER = (
    ("E1", 0), ("E2", 0), ("E1", 2), ("E1", 1), ("E1", 3), ("E5", 0), ("E3", 0), ("E6", 0), ("E4", 0),
    ("E7", 0), ("O1", 0), ("E5", 1), ("E3", 1), ("E6", 1), ("E2", 1), ("E4", 1), ("P1", 0), ("E3", 2),
    ("P2", 0), ("E7", 1), ("P3", 0), ("P4", 0), ("E5", 2), ("O2", 0), ("E3", 3), ("E6", 2), ("E2", 2),
    ("E4", 2), ("E2", 3), ("O1", 1), ("P1", 1), ("P2", 1), ("P3", 1), ("E7", 2), ("P4", 1), ("E5", 3),
    ("E6", 3), ("O3", 0), ("O1", 2), ("F0", 0), ("E7", 3), ("P1", 2), ("P2", 2), ("O2", 2), ("F2b", 0),
    ("F2", 0), ("P3", 2), ("E4", 3), ("O2", 1), ("P4", 2), ("O3", 1), ("F0", 1), ("F3", 0), ("P1", 3),
    ("P2", 3), ("P3", 3), ("P4", 3), ("F4", 0), ("F2", 1), ("O1", 3), ("O3", 2), ("F0", 2), ("G2", 0),
    ("O2", 3), ("G5", 0), ("F2b", 1), ("O3", 3), ("F0", 3), ("F2", 2), ("F3", 1), ("G3", 0), ("G4", 0),
    ("F4", 1), ("F2", 3), ("G7", 0), ("F3", 2), ("G6", 0), ("B1", 0), ("B2", 0), ("G2", 1), ("F2b", 2),
    ("G3", 1), ("B3", 0), ("B4", 0), ("F2b", 3), ("G5", 1), ("F3", 3), ("F4", 2), ("G4", 1), ("F4", 3),
    ("G2", 2), ("G7", 1), ("G6", 1), ("G3", 2), ("G5", 2), ("B1", 1), ("G2", 3), ("G5", 3), ("G4", 2),
    ("S2b", 0), ("G3", 3), ("B2", 1), ("B3", 1), ("B4", 1), ("S2", 0), ("G6", 2), ("G4", 3), ("G7", 2),
    ("B1", 2), ("B2", 2), ("G6", 3), ("B3", 2), ("B4", 2), ("G7", 3), ("S2", 1), ("B1", 3), ("B2", 3),
    ("B3", 3), ("WG", 1), ("WG", 4), ("S2b", 2), ("WG", 2), ("B4", 3), ("S3", 0), ("S2", 2), ("WU", 1),
    ("WU", 5), ("WU", 2), ("S2", 3), ("WG", 3), ("K1", 0), ("S3", 1), ("WU", 3), ("WG", 0), ("S2b", 3),
    ("WG", 5), ("S4", 0), ("S2b", 1), ("S3", 2), ("WD", 0), ("S3", 3), ("WU", 4), ("WD", 1), ("WU", 0),
    ("WD", 2), ("K2", 0), ("S4", 3), ("S4", 2), ("S4", 1),
)


def dot_nn(a, b):
    return jnp.dot(a, b, preferred_element_type=F32)


def dot_nt(a, b):
    return lax.dot_general(a, b, (((1,), (1,)), ((), ())), preferred_element_type=F32)


def dot_tn(a, b):
    return lax.dot_general(a, b, (((0,), (0,)), ((), ())), preferred_element_type=F32)


def blocks(total, size, body):
    @pl.loop(0, total // size)
    def _(i):
        body(pl.multiple_of(i * size, size))


def kernel(
    tokens, upstream, gate_w, up_w, down_w, gain, stale_gate, stale_up, stale_down, stale_gain,
    out_tokens, out_gate, out_up, out_down, out_gain,
    wg, wu, wd, sg, su, sd, ups, tok, tok_next, x, xs, inv, gv, uv, gt, ut, hid, hid_s,
    gap, peer, rs1, rs2, go, ggp, gup, outt, acc, acc_in, gain_buf,
    send, recv, local,
):
    member = lax.axis_index("member")
    j = lax.axis_index("fsdp")
    y, z = j // 4, j % 4
    members = lax.axis_size("member")
    z_up, z_dn, z_far = (z + 1) % 4, (z + 3) % 4, (z + 2) % 4
    other = 1 - y
    UP, DN, ACROSS = (member, y * 4 + z_up), (member, y * 4 + z_dn), (member, other * 4 + z)
    NEXT = ((member + 1) % members, j)
    PREV = ((member + members - 1) % members, j)
    edge_prev, edge_next = ((member + 7) % 8) // 7, (member % 8) // 7
    PREV_X = (PREV[0], ((y + edge_prev) % 2) * 4 + z)
    NEXT_X = (NEXT[0], ((y + edge_next) % 2) * 4 + z)

    pos = {
        "o": j,
        "ou": y * 4 + z_up,
        "od": y * 4 + z_dn,
        "of": y * 4 + z_far,
        "x": other * 4 + z,
        "xu": other * 4 + z_up,
        "xd": other * 4 + z_dn,
        "xf": other * 4 + z_far,
    }

    def rows(b, chunk):
        return pl.ds(pl.multiple_of(b * M + pos[chunk] * RB, 16), RB)

    def batch(b):
        return pl.ds(b * M, M)

    numbers = {}

    def number(key):
        return numbers.setdefault(key, len(numbers))

    def remote(key, src, dst, device):
        i = number(key)
        return pltpu.make_async_remote_copy(
            src_ref=src,
            dst_ref=dst,
            send_sem=send.at[i],
            recv_sem=recv.at[i],
            device_id=device,
            device_id_type=MESH,
        )

    sent = []

    def start(key, src, dst, device):
        copy = remote(key, src, dst, device)
        copy.start()
        sent.append((key, copy))

    def arrive(key, dst, device):
        remote(key, dst, dst, device).wait_recv()

    locals_ = {}

    def fetch(key, src, dst):
        copy = pltpu.make_async_copy(src, dst, local.at[len(locals_)])
        locals_[key] = copy
        copy.start()

    done = set()

    def need(key):
        if key not in done:
            done.add(key)
            locals_[key].wait()

    barrier = pltpu.get_barrier_semaphore()
    for step in range(1, N):
        pl.semaphore_signal(barrier, inc=1, device_id=(member, (j + step) % N), device_id_type=MESH)
    for to in (NEXT[0], PREV[0]):
        for at in (y, other):
            pl.semaphore_signal(barrier, inc=1, device_id=(to, at * 4 + z), device_id_type=MESH)
    for b in range(NB):
        fetch(("t", b), tokens.at[0, pl.ds(b * RB, RB)], tok.at[rows(b, "o")])
    fetch("sg", stale_gate.at[0], sg)
    fetch("su", stale_up.at[0], su)
    fetch("sd", stale_down.at[0], sd)
    fetch("wg", gate_w.at[0], wg)
    fetch("wu", up_w.at[0], wu)
    fetch("wd", down_w.at[0], wd)
    fetch("ups", upstream.at[0], ups)
    acc[...] = jnp.zeros_like(acc)
    pl.semaphore_wait(barrier, N + 3)

    mirror = {"ou": "od", "od": "ou", "xu": "xd", "xd": "xu"}

    def side(b, chunk):
        return mirror.get(chunk, chunk) if b % 2 else chunk

    def ways(b):
        return (DN, UP) if b % 2 else (UP, DN)

    def onward(b, chunk):
        chunk = side(b, chunk)
        if chunk[0] == "o":
            start(("n", b, chunk), tok.at[rows(b, chunk)], tok_next.at[rows(b, chunk)], PREV)
        else:
            at = ((other + edge_prev) % 2) * 4 + pos[chunk] % 4
            r = pl.ds(pl.multiple_of(b * M + at * RB, 16), RB)
            start(("n", b, chunk), tok.at[r], tok_next.at[r], PREV_X)

    def gather(name, ref, then, crossings):
        def move(b, chunk, way, device):
            r = rows(b, side(b, chunk))
            start((name, b, chunk, way), ref.at[r], ref.at[r], device)

        def got(b, chunk, sent_as, way):
            arrive((name, b, sent_as, way), ref.at[rows(b, side(b, chunk))], UP)

        def e1(b):
            up, dn = ways(b)
            if name == "g":
                move(b, "o", "a", ACROSS)
            elif b == 0:
                for each in range(NB):
                    need(("t", each))
                    move(each, "o", "a", ACROSS)
                    if each == 0:
                        move(b, "o", "u", up)
                        move(b, "o", "d", dn)
                for each in range(NB):
                    then(each, "o")
                return
            move(b, "o", "u", up)
            move(b, "o", "d", dn)

        def e2(b):
            got(b, "od", "o", "u")
            if crossings == 2:
                move(b, "od", "a", ACROSS)
            move(b, "od", "u", ways(b)[0])
            then(b, "od")

        def e3(b):
            got(b, "x", "o", "a")
            move(b, "x", "d", ways(b)[1])
            if crossings == 1:
                move(b, "x", "u", ways(b)[0])
            then(b, "x")

        def e4(b):
            if crossings == 2:
                got(b, "xd", "od", "a")
                move(b, "xd", "u", ways(b)[0])
            else:
                got(b, "xd", "x", "u")
            then(b, "xd")

        def e5(b):
            got(b, "ou", "o", "d")
            then(b, "ou")

        def e6(b):
            got(b, "xu", "x", "d")
            if crossings == 1:
                move(b, "xu", "d", ways(b)[1])
            then(b, "xu")

        def e7(b):
            got(b, "of", "od", "u")
            if crossings == 2:
                got(b, "xf", "xd", "u")
            else:
                got(b, "xf", "xu", "d")
            then(b, "of")
            then(b, "xf")

        return e1, e2, e3, e4, e5, e6, e7

    def scatter(name, ref, land):
        def slot(b, k):
            return land.at[pl.ds((b * 7 + k) * RB, RB)]

        def push(b, chunk, k, device):
            start((name, b, k), ref.at[rows(b, side(b, chunk))], slot(b, k), device)

        def merge(b, chunk, slots, k, device):
            for each in slots:
                arrive((name, b, each), slot(b, each), UP)
            total = ref[rows(b, side(b, chunk)), :].astype(F32)
            for each in slots:
                total = total + slot(b, each)[...].astype(F32)
            at = slot(b, slots[0])
            at[...] = total.astype(BF16)
            start((name, b, k), at, slot(b, k), device)

        def f1(b):
            up, dn = ways(b)
            push(b, "xf", 0, dn)
            push(b, "xu", 2, up)
            push(b, "of", 1, dn)
            push(b, "ou", 3, up)

        def f2(b):
            merge(b, "xd", (0,), 4, ACROSS)

        def f2b(b):
            merge(b, "x", (2,), 5, ACROSS)

        def f3(b):
            merge(b, "od", (1, 4), 6, ways(b)[1])

        def f4(b):
            for k in (3, 5, 6):
                arrive((name, b, k), slot(b, k), UP)

        def result(b, first, size):
            at = pl.multiple_of(b * M + j * RB + first, 16)
            total = ref[pl.ds(at, size), :].astype(F32)
            for k in (3, 5, 6):
                total = total + land[pl.ds((b * 7 + k) * RB + first, size), :].astype(F32)
            return total

        return f1, f2, f2b, f3, f4, result

    ea = gather("a", tok, onward, 1)
    eg = gather("g", go, lambda b, chunk: None, 2)
    ra = scatter("r", gap, rs1)
    rg = scatter("s", peer, rs2)

    gain_row = gain[...].astype(F32)
    stale_row = stale_gain[...].astype(F32)

    def normalize(src, dst, at_dst, b, factor, keep):
        def body(at):
            values = src[pl.ds(pl.multiple_of(b * M + at, 16), 16), :].astype(F32)
            scale = lax.rsqrt(jnp.mean(values * values, axis=-1, keepdims=True) + EPS)
            dst[pl.ds(pl.multiple_of(at_dst + at, 16), 16), :] = (values * scale * factor).astype(BF16)
            if keep:
                inv[pl.ds(pl.multiple_of(b * M + at, 16), 16), :] = scale

        blocks(M, 16, body)

    def activate(g_ref, u_ref, base, dst, at_dst):
        def body(at):
            g = g_ref[pl.ds(pl.multiple_of(base + at, 16), 16), :]
            u = u_ref[pl.ds(pl.multiple_of(base + at, 16), 16), :]
            dst[pl.ds(pl.multiple_of(at_dst + at, 16), 16), :] = (g * jax.nn.sigmoid(g) * u).astype(BF16)

        blocks(M, 16, body)

    def p1(b):
        for chunk in pos:
            arrive(("n", b, chunk), tok_next.at[rows(b, chunk)], PREV)
        normalize(tok_next, xs, 0, b, stale_row, False)

    def p2(b):
        need("sg")
        gt[...] = dot_nn(xs[...], sg[...])

    def p3(b):
        need("su")
        ut[...] = dot_nn(xs[...], su[...])
        activate(gt, ut, 0, hid_s, 0)

    def p4(b):
        need("sd")
        peer[batch(b), :] = dot_nn(hid_s[...], sd[...]).astype(BF16)
        for half, device in ((0, NEXT), (1, NEXT_X)):
            r = pl.ds(b * M + half * (M // 2), M // 2)
            start(("p", b, half), peer.at[r], gap.at[r], device)

    def o1(b):
        normalize(tok, x, b * M, b, gain_row, True)

    def o2(b):
        need("wg")
        gv[batch(b), :] = dot_nn(x[batch(b), :], wg[...])

    def o3(b):
        need("wu")
        uv[batch(b), :] = dot_nn(x[batch(b), :], wu[...])
        activate(gv, uv, b * M, hid, b * M)

    def f0(b):
        need("wd")
        for half in range(2):
            arrive(("p", b, half), gap.at[pl.ds(b * M + half * (M // 2), M // 2)], PREV)
        own = dot_nn(hid[batch(b), :], wd[...])
        gap[batch(b), :] = (own - gap[batch(b), :].astype(F32)).astype(BF16)
        ra[0](b)

    def f4(b):
        need("ups")
        ra[4](b)
        for first in range(0, RB, 16):
            total = ra[5](b, first, 16)
            mine = ups[pl.ds(b * RB + first, 16), :].astype(F32) + AGREE * total
            go[pl.ds(pl.multiple_of(b * M + j * RB + first, 16), 16), :] = mine.astype(BF16)
        eg[0](b)

    def b1(b):
        gt[...] = dot_nt(go[batch(b), :], wd[...])

        def body(at):
            g = gv[pl.ds(pl.multiple_of(b * M + at, 16), 16), :]
            s = jax.nn.sigmoid(g)
            gh = gt[pl.ds(at, 16), :]
            u = uv[pl.ds(pl.multiple_of(b * M + at, 16), 16), :]
            ggp[pl.ds(pl.multiple_of(b * M + at, 16), 16), :] = (gh * u * s * (1.0 + g * (1.0 - s))).astype(BF16)
            gup[pl.ds(pl.multiple_of(b * M + at, 16), 16), :] = (gh * (g * s)).astype(BF16)

        blocks(M, 16, body)

    def back(b, half):
        if half == 0:
            for key, copy in sent:
                if key[:2] == ("p", b):
                    copy.wait_send()
                    waited.add(key)
        cols = pl.ds(half * FB, FB)
        total = dot_nt(ggp[batch(b), :], wg[cols, :]) + dot_nt(gup[batch(b), :], wu[cols, :])
        peer[batch(b), cols] = total.astype(BF16)

    waited = set()

    def b2(b):
        back(b, 0)

    def b3(b):
        back(b, 1)
        rg[0](b)

    def b4(b):
        def body(at):
            r = pl.ds(pl.multiple_of(b * M + at, 16), 16)
            part = part_of[r, :].astype(F32) * (tok[r, :].astype(F32) * inv[r, :])
            acc[...] += part[:8] + part[8:]

        part_of = peer
        blocks(M, 16, body)

    def k1(b):
        for step in range(1, N):
            start(("k", step), acc, acc_in.at[step], (member, (j + step) % N))

    def k2(b):
        total = acc[...]
        for step in range(1, N):
            arrive(("k", step), acc_in.at[step], (member, (j + step) % N))
            total = total + acc_in[step]
        gain_buf[...] = jnp.sum(total, axis=0, keepdims=True)
        fetch("ok", gain_buf, out_gain)

    def f4g(b):
        rg[4](b)
        for first in range(0, RB, 16):
            grad_in = rg[5](b, first, 16)
            r = pl.ds(pl.multiple_of(b * M + j * RB + first, 16), 16)
            scale = inv[r, :]
            normed = tok[r, :].astype(F32) * scale
            grad_normed = grad_in * gain_row
            mean = jnp.mean(grad_normed * normed, axis=-1, keepdims=True)
            outt[pl.ds(b * RB + first, 16), :] = (
                go[r, :].astype(F32) + scale * (grad_normed - normed * mean)
            ).astype(BF16)
        fetch(("ot", b), outt.at[pl.ds(b * RB, RB)], out_tokens.at[0, pl.ds(b * RB, RB)])

    def weight(name, left, right, dst, out, size):
        def task(i):
            r = pl.ds(i * size, size)
            dst[r, :] = dot_tn(left[:, i * size : (i + 1) * size], right[...]).astype(BF16)
            fetch((name, i), dst.at[r], out.at[0, r])

        return task

    tasks = {
        "P1": p1, "P2": p2, "P3": p3, "P4": p4, "O1": o1, "O2": o2, "O3": o3, "F0": f0, "F4": f4,
        "F2": ra[1], "F2b": ra[2], "F3": ra[3], "S2": rg[1], "S2b": rg[2], "S3": rg[3], "S4": f4g,
        "B1": b1, "B2": b2, "B3": b3, "B4": b4, "K1": k1, "K2": k2,
        "WD": weight("wd", hid, go, sd, out_down, 256),
        "WG": weight("wg", x, ggp, sg, out_gate, 256),
        "WU": weight("wu", x, gup, su, out_up, 256),
    }
    for i in range(7):
        tasks["E%d" % (i + 1)] = ea[i]
        tasks["G%d" % (i + 1)] = eg[i]
    for name, index in ORDER:
        tasks[name](index)

    for key, copy in sent:
        if key not in waited:
            copy.wait_send()
    for key in locals_:
        need(key)


def hand_over(*refs):
    sources, results, holds, sems = refs[:5], refs[5:10], refs[10:15], refs[15]
    steps = []
    for i, (src, hold, dst) in enumerate(zip(sources, holds, results)):
        whole = src.shape[1]
        parts = 4 if 0 < i < 4 else 1
        for part in range(parts):
            r = pl.ds(part * (whole // parts), whole // parts)
            steps.append((
                pltpu.make_async_copy(src.at[:, r], hold.at[:, r], sems.at[0, i, part]),
                pltpu.make_async_copy(hold.at[:, r], dst.at[:, r], sems.at[1, i, part]),
            ))
    for first, _ in steps:
        first.start()
    for first, second in steps:
        first.wait()
        second.start()
    for _, second in steps:
        second.wait()


def shards(
    tokens, upstream, gate_weight, up_weight, down_weight, norm_gain,
    stale_gate, stale_up, stale_down, stale_gain,
):
    hbm = pl.BlockSpec(memory_space=pl.ANY)
    vmem = pl.BlockSpec(memory_space=pltpu.VMEM)
    total = N * ROWS
    wide = pltpu.VMEM((total, D), BF16)
    narrow = pltpu.VMEM((total, FB), F32)
    half = pltpu.VMEM((total, FB), BF16)
    tall = pltpu.VMEM((D, FB), BF16)
    flat = pltpu.VMEM((FB, D), BF16)
    step = pltpu.VMEM((M, FB), F32)
    land = pltpu.VMEM((NB * 7 * RB, D), BF16)
    results = (
        jax.ShapeDtypeStruct((1, ROWS, D), BF16),
        jax.ShapeDtypeStruct((1, D, FB), BF16),
        jax.ShapeDtypeStruct((1, D, FB), BF16),
        jax.ShapeDtypeStruct((1, FB, D), BF16),
        jax.ShapeDtypeStruct((1, D), F32),
    )
    parts = pl.pallas_call(
        kernel,
        out_shape=results,
        in_specs=[hbm, hbm, hbm, hbm, hbm, vmem, hbm, hbm, hbm, vmem],
        out_specs=(hbm,) * 5,
        scratch_shapes=[
            tall, tall, flat, tall, tall, flat,
            pltpu.VMEM((ROWS, D), BF16),
            wide, wide, wide,
            pltpu.VMEM((M, D), BF16),
            pltpu.VMEM((total, 1), F32),
            narrow, narrow, step, step, half,
            pltpu.VMEM((M, FB), BF16),
            wide, wide, land, land, wide, half, half,
            pltpu.VMEM((ROWS, D), BF16),
            pltpu.VMEM((8, D), F32),
            pltpu.VMEM((N, 8, D), F32),
            pltpu.VMEM((1, D), F32),
            pltpu.SemaphoreType.DMA((NB * 38 + 8,)),
            pltpu.SemaphoreType.DMA((NB * 38 + 8,)),
            pltpu.SemaphoreType.DMA((2 * NB + 7 + 16,)),
        ],
        compiler_params=pltpu.CompilerParams(
            collective_id=0, has_side_effects=True, vmem_limit_bytes=62 * 2**20
        ),
        name="layer",
    )(
        tokens, upstream, gate_weight, up_weight, down_weight, norm_gain,
        stale_gate, stale_up, stale_down, stale_gain,
    )
    return pl.pallas_call(
        hand_over,
        out_shape=results,
        in_specs=[hbm] * 5,
        out_specs=(hbm,) * 5,
        scratch_shapes=[pltpu.VMEM(r.shape, r.dtype) for r in results]
        + [pltpu.SemaphoreType.DMA((2, 5, 4))],
        compiler_params=pltpu.CompilerParams(vmem_limit_bytes=62 * 2**20),
        name="hand_over",
    )(*parts)


def solution(mesh):
    in_specs = (
        P("member", "fsdp", None),
        P("member", "fsdp", None),
        P("member", None, "fsdp"),
        P("member", None, "fsdp"),
        P("member", "fsdp", None),
        P("member", None),
        P("member", None, "fsdp"),
        P("member", None, "fsdp"),
        P("member", "fsdp", None),
        P("member", None),
    )
    out_specs = (
        P("member", "fsdp", None),
        P("member", None, "fsdp"),
        P("member", None, "fsdp"),
        P("member", "fsdp", None),
        P("member", None),
    )
    return jax.shard_map(shards, mesh=mesh, in_specs=in_specs, out_specs=out_specs, check_vma=False)
```

```python
import functools
import jax
import jax.numpy as jnp
from jax import lax
from jax.experimental import pallas as pl
from jax.experimental.pallas import tpu as pltpu
from jax.sharding import PartitionSpec as P

EPS = 1e-05
AGREE = 1.0
MESH = pl.DeviceIdType.MESH
F32 = jnp.float32
BF16 = jnp.bfloat16
D = 1536
FB = 768
N = 8
ROWS = 128
NB = 4
RB = ROWS // NB
KR, KG, KS = 1, 2, 2
M = N * RB

ORDER = [('E1', 0), ('E1', 1), ('E2', 0), ('E3', 0), ('E5', 0), ('E5', 1), ('N', 1), ('E6', 0), ('E3', 1), ('E4', 0), ('E7', 0), ('E6', 1), ('E1', 2), ('E2', 1), ('E1', 3), ('N', 2), ('E3', 2), ('O1', 0), ('O2', 0), ('E3', 3), ('P1', 0), ('P2', 0), ('E7', 1), ('P3', 0), ('P4', 0), ('E4', 1), ('E2', 2), ('O1', 1), ('E5', 2), ('E6', 2), ('E2', 3), ('O3', 0), ('P1', 1), ('P2', 1), ('E7', 2), ('E4', 2), ('E5', 3), ('E6', 3), ('N', 3), ('P3', 1), ('P4', 1), ('O1', 2), ('E4', 3), ('E7', 3), ('F0', 0), ('P1', 2), ('P2', 2), ('O2', 1), ('P3', 2), ('P4', 2), ('F2b', 0), ('F2', 0), ('O3', 1), ('F0', 1), ('P1', 3), ('P2', 3), ('F3', 0), ('P3', 3), ('O2', 2), ('F2', 1), ('P4', 3), ('F2b', 1), ('O3', 2), ('F0', 2), ('F3', 1), ('F4', 0), ('F2', 2), ('O1', 3), ('F2b', 2), ('O2', 3), ('O3', 3), ('F0', 3), ('F2', 3), ('G2', 0), ('F4', 1), ('F3', 2), ('G4', 0), ('G3', 0), ('G2', 1), ('F3', 3), ('G5', 1), ('G5', 0), ('G3', 1), ('G6', 0), ('G7', 0), ('F4', 2), ('B1', 0), ('F2b', 3), ('G6', 1), ('G4', 1), ('G2', 2), ('F4', 3), ('G7', 1), ('B2', 0), ('G3', 2), ('G4', 2), ('B3', 0), ('G5', 3), ('G2', 3), ('B1', 1), ('G5', 2), ('B2', 1), ('B4', 0), ('G6', 2), ('G7', 2), ('S2', 0), ('G3', 3), ('B1', 2), ('G4', 3), ('B3', 1), ('S2b', 0), ('B4', 1), ('B2', 2), ('G6', 3), ('B3', 2), ('G7', 3), ('B1', 3), ('WG', 0), ('S2', 1), ('S2b', 1), ('WU', 1), ('B2', 3), ('B3', 3), ('WG', 3), ('WG', 4), ('WG', 1), ('S2', 2), ('WG', 5), ('WD', 1), ('WU', 4), ('S2', 3), ('B4', 3), ('S3', 1), ('S2b', 2), ('WU', 0), ('S3', 0), ('B4', 2), ('WU', 2), ('S3', 2), ('K1', 0), ('S3', 3), ('S2b', 3), ('WU', 5), ('WG', 2), ('S4', 1), ('WD', 2), ('WD', 0), ('WU', 3), ('S4', 0), ('S4', 3), ('K2', 0), ('S4', 2)]


def dot_nn(a, b):
    return jnp.dot(a, b, preferred_element_type=F32)


def dot_nt(a, b):
    return lax.dot_general(a, b, (((1,), (1,)), ((), ())), preferred_element_type=F32)


def dot_tn(a, b):
    return lax.dot_general(a, b, (((0,), (0,)), ((), ())), preferred_element_type=F32)


def blocks(total, size, body):
    @pl.loop(0, total // size)
    def _(i):
        body(pl.multiple_of(i * size, size))


def kernel(
    tokens, upstream, gate_w, up_w, down_w, gain, stale_gate, stale_up, stale_down, stale_gain,
    out_tokens, out_gate, out_up, out_down, out_gain,
    wg, wu, wd, sg, su, sd, ups, tok, tok_next, x, xs, inv, gv, uv, gt, ut, hid, hid_s,
    gap, peer, rs1, rs2, go, ggp, gup, outt, acc, acc_out, acc_in, gain_buf,
    send, recv, local,
):
    member = lax.axis_index("member")
    j = lax.axis_index("fsdp")
    y, z = j // 4, j % 4
    members = lax.axis_size("member")
    z_up, z_dn, z_far = (z + 1) % 4, (z + 3) % 4, (z + 2) % 4
    other = 1 - y
    UP, DN, ACROSS = (member, y * 4 + z_up), (member, y * 4 + z_dn), (member, other * 4 + z)
    NEXT = ((member + 1) % members, j)
    PREV = ((member + members - 1) % members, j)
    edge_prev, edge_next = ((member + 7) % 8) // 7, (member % 8) // 7
    PREV_X = (PREV[0], ((y + edge_prev) % 2) * 4 + z)
    NEXT_X = (NEXT[0], ((y + edge_next) % 2) * 4 + z)

    pos = {
        "o": j,
        "ou": y * 4 + z_up,
        "od": y * 4 + z_dn,
        "of": y * 4 + z_far,
        "x": other * 4 + z,
        "xu": other * 4 + z_up,
        "xd": other * 4 + z_dn,
        "xf": other * 4 + z_far,
    }

    def rows(b, chunk):
        return pl.ds(pl.multiple_of(b * M + pos[chunk] * RB, 16), RB)

    def batch(b):
        return pl.ds(b * M, M)

    numbers = {}

    def number(key):
        return numbers.setdefault(key, len(numbers))

    def remote(key, src, dst, device):
        i = number(key)
        return pltpu.make_async_remote_copy(
            src_ref=src,
            dst_ref=dst,
            send_sem=send.at[i],
            recv_sem=recv.at[i],
            device_id=device,
            device_id_type=MESH,
        )

    sent = []

    def start(key, src, dst, device):
        copy = remote(key, src, dst, device)
        copy.start()
        sent.append((key, copy))

    def arrive(key, dst, device):
        remote(key, dst, dst, device).wait_recv()

    locals_ = {}

    def fetch(key, src, dst):
        copy = pltpu.make_async_copy(src, dst, local.at[len(locals_)])
        locals_[key] = copy
        copy.start()

    done = set()

    def need(key):
        if key not in done:
            done.add(key)
            locals_[key].wait()

    barrier = pltpu.get_barrier_semaphore()
    for step in range(1, N):
        pl.semaphore_signal(barrier, inc=1, device_id=(member, (j + step) % N), device_id_type=MESH)
    for to in (NEXT[0], PREV[0]):
        for at in (y, other):
            pl.semaphore_signal(barrier, inc=1, device_id=(to, at * 4 + z), device_id_type=MESH)
    for b in range(NB):
        fetch(("t", b), tokens.at[0, pl.ds(b * RB, RB)], tok.at[rows(b, "o")])
    fetch("sg", stale_gate.at[0], sg)
    fetch("su", stale_up.at[0], su)
    fetch("sd", stale_down.at[0], sd)
    fetch("wg", gate_w.at[0], wg)
    fetch("wu", up_w.at[0], wu)
    fetch("wd", down_w.at[0], wd)
    fetch("ups", upstream.at[0], ups)
    acc[...] = jnp.zeros_like(acc)
    pl.semaphore_wait(barrier, N + 3)

    mirror = {"ou": "od", "od": "ou", "xu": "xd", "xd": "xu"}

    def side(b, chunk):
        return mirror.get(chunk, chunk) if b % 2 else chunk

    def ways(b):
        return (DN, UP) if b % 2 else (UP, DN)

    def onward(b, chunk):
        chunk = side(b, chunk)
        if chunk[0] == "o":
            start(("n", b, chunk), tok.at[rows(b, chunk)], tok_next.at[rows(b, chunk)], PREV)
        else:
            at = ((other + edge_prev) % 2) * 4 + pos[chunk] % 4
            r = pl.ds(pl.multiple_of(b * M + at * RB, 16), RB)
            start(("n", b, chunk), tok.at[r], tok_next.at[r], PREV_X)

    def gather(name, ref, then, crossings):
        def move(b, chunk, way, device):
            r = rows(b, side(b, chunk))
            start((name, b, chunk, way), ref.at[r], ref.at[r], device)

        def got(b, chunk, sent_as, way):
            arrive((name, b, sent_as, way), ref.at[rows(b, side(b, chunk))], UP)

        def e1(b):
            up, dn = ways(b)
            if name == "g":
                move(b, "o", "a", ACROSS)
            elif b == 0:
                for each in range(NB):
                    need(("t", each))
                    move(each, "o", "a", ACROSS)
                    if each == 0:
                        move(b, "o", "u", up)
                        move(b, "o", "d", dn)
                then(b, "o")
                return
            move(b, "o", "u", up)
            move(b, "o", "d", dn)

        def e2(b):
            got(b, "od", "o", "u")
            if crossings == 2:
                move(b, "od", "a", ACROSS)
            move(b, "od", "u", ways(b)[0])
            then(b, "od")

        def e3(b):
            got(b, "x", "o", "a")
            move(b, "x", "d", ways(b)[1])
            if crossings == 1:
                move(b, "x", "u", ways(b)[0])
            then(b, "x")

        def e4(b):
            if crossings == 2:
                got(b, "xd", "od", "a")
                move(b, "xd", "u", ways(b)[0])
            else:
                got(b, "xd", "x", "u")
            then(b, "xd")

        def e5(b):
            got(b, "ou", "o", "d")
            then(b, "ou")

        def e6(b):
            got(b, "xu", "x", "d")
            if crossings == 1:
                move(b, "xu", "d", ways(b)[1])
            then(b, "xu")

        def e7(b):
            got(b, "of", "od", "u")
            if crossings == 2:
                got(b, "xf", "xd", "u")
            else:
                got(b, "xf", "xu", "d")
            then(b, "of")
            then(b, "xf")

        return e1, e2, e3, e4, e5, e6, e7

    def scatter(name, ref, land, crossings):
        def slot(b, k):
            return land.at[pl.ds((b * 7 + k) * RB, RB)]

        def push(b, chunk, k, device):
            start((name, b, k), ref.at[rows(b, side(b, chunk))], slot(b, k), device)

        def merge(b, chunk, slots, k, device):
            for each in slots:
                arrive((name, b, each), slot(b, each), UP)
            total = ref[rows(b, side(b, chunk)), :].astype(F32)
            for each in slots:
                total = total + slot(b, each)[...].astype(F32)
            at = slot(b, slots[0])
            at[...] = total.astype(BF16)
            start((name, b, k), at, slot(b, k), device)

        last = (3, 5, 6) if crossings == 2 else (2, 5, 6)

        def f1(b):
            up, dn = ways(b)
            if crossings == 2:
                push(b, "xf", 0, dn)
                push(b, "xu", 2, up)
                push(b, "of", 1, dn)
                push(b, "ou", 3, up)
            else:
                push(b, "xf", 0, up)
                push(b, "xd", 3, dn)
                push(b, "of", 1, dn)
                push(b, "ou", 2, up)

        def f2(b):
            if crossings == 2:
                merge(b, "xd", (0,), 4, ACROSS)
            else:
                merge(b, "xu", (0,), 4, ways(b)[0])

        def f2b(b):
            if crossings == 2:
                merge(b, "x", (2,), 5, ACROSS)
            else:
                merge(b, "od", (1,), 5, ways(b)[1])

        def f3(b):
            if crossings == 2:
                merge(b, "od", (1, 4), 6, ways(b)[1])
            else:
                merge(b, "x", (3, 4), 6, ACROSS)

        def f4(b):
            for k in last:
                arrive((name, b, k), slot(b, k), UP)

        def result(b, first, size):
            at = pl.multiple_of(b * M + j * RB + first, 16)
            total = ref[pl.ds(at, size), :].astype(F32)
            for k in last:
                total = total + land[pl.ds((b * 7 + k) * RB + first, size), :].astype(F32)
            return total

        return f1, f2, f2b, f3, f4, result

    ea = gather("a", tok, onward, 1)
    eg = gather("g", go, lambda b, chunk: None, KG)
    ra = scatter("r", gap, rs1, KR)
    rg = scatter("s", peer, rs2, KS)

    gain_row = gain[...].astype(F32)
    stale_row = stale_gain[...].astype(F32)

    def normalize(src, dst, at_dst, b, factor, keep):
        def body(at):
            values = src[pl.ds(pl.multiple_of(b * M + at, 16), 16), :].astype(F32)
            scale = lax.rsqrt(jnp.mean(values * values, axis=-1, keepdims=True) + EPS)
            dst[pl.ds(pl.multiple_of(at_dst + at, 16), 16), :] = (values * scale * factor).astype(BF16)
            if keep:
                inv[pl.ds(pl.multiple_of(b * M + at, 16), 16), :] = scale

        blocks(M, 16, body)

    def activate(g_ref, u_ref, base, dst, at_dst):
        def body(at):
            g = g_ref[pl.ds(pl.multiple_of(base + at, 16), 16), :]
            u = u_ref[pl.ds(pl.multiple_of(base + at, 16), 16), :]
            dst[pl.ds(pl.multiple_of(at_dst + at, 16), 16), :] = (g * jax.nn.sigmoid(g) * u).astype(BF16)

        blocks(M, 16, body)

    def p1(b):
        for chunk in pos:
            arrive(("n", b, chunk), tok_next.at[rows(b, chunk)], PREV)
        normalize(tok_next, xs, 0, b, stale_row, False)

    def p2(b):
        need("sg")
        gt[...] = dot_nn(xs[...], sg[...])

    def p3(b):
        need("su")
        ut[...] = dot_nn(xs[...], su[...])
        activate(gt, ut, 0, hid_s, 0)

    def p4(b):
        need("sd")
        peer[batch(b), :] = dot_nn(hid_s[...], sd[...]).astype(BF16)
        for half, device in ((0, NEXT), (1, NEXT_X)):
            r = pl.ds(b * M + half * (M // 2), M // 2)
            start(("p", b, half), peer.at[r], gap.at[r], device)

    def o1(b):
        normalize(tok, x, b * M, b, gain_row, True)

    def o2(b):
        need("wg")
        gv[batch(b), :] = dot_nn(x[batch(b), :], wg[...])

    def o3(b):
        need("wu")
        uv[batch(b), :] = dot_nn(x[batch(b), :], wu[...])
        activate(gv, uv, b * M, hid, b * M)

    def f0(b):
        need("wd")
        for half in range(2):
            arrive(("p", b, half), gap.at[pl.ds(b * M + half * (M // 2), M // 2)], PREV)
        own = dot_nn(hid[batch(b), :], wd[...])
        gap[batch(b), :] = (own - gap[batch(b), :].astype(F32)).astype(BF16)
        ra[0](b)

    def f4(b):
        need("ups")
        ra[4](b)
        for first in range(0, RB, 16):
            total = ra[5](b, first, 16)
            mine = ups[pl.ds(b * RB + first, 16), :].astype(F32) + AGREE * total
            go[pl.ds(pl.multiple_of(b * M + j * RB + first, 16), 16), :] = mine.astype(BF16)
        eg[0](b)

    def b1(b):
        gt[...] = dot_nt(go[batch(b), :], wd[...])

        def body(at):
            g = gv[pl.ds(pl.multiple_of(b * M + at, 16), 16), :]
            s = jax.nn.sigmoid(g)
            gh = gt[pl.ds(at, 16), :]
            u = uv[pl.ds(pl.multiple_of(b * M + at, 16), 16), :]
            ggp[pl.ds(pl.multiple_of(b * M + at, 16), 16), :] = (gh * u * s * (1.0 + g * (1.0 - s))).astype(BF16)
            gup[pl.ds(pl.multiple_of(b * M + at, 16), 16), :] = (gh * (g * s)).astype(BF16)

        blocks(M, 16, body)

    def back(b, half):
        if half == 0:
            for key, copy in sent:
                if key[:2] == ("p", b):
                    copy.wait_send()
                    waited.add(key)
        cols = pl.ds(half * FB, FB)
        total = dot_nt(ggp[batch(b), :], wg[cols, :]) + dot_nt(gup[batch(b), :], wu[cols, :])
        peer[batch(b), cols] = total.astype(BF16)

    waited = set()

    def b2(b):
        back(b, 0)

    def b3(b):
        back(b, 1)
        rg[0](b)

    def b4(b):
        def body(at):
            r = pl.ds(pl.multiple_of(b * M + at, 16), 16)
            part = part_of[r, :].astype(F32) * (tok[r, :].astype(F32) * inv[r, :])
            acc[...] += part[:8] + part[8:]

        part_of = peer
        blocks(M, 16, body)

    def k1(b):
        acc_out[...] = jnp.sum(acc[...], axis=0, keepdims=True)
        for step in range(1, N):
            start(("k", step), acc_out, acc_in.at[step], (member, (j + step) % N))

    def k2(b):
        total = acc_out[...]
        for step in range(1, N):
            arrive(("k", step), acc_in.at[step], (member, (j + step) % N))
            total = total + acc_in[step]
        gain_buf[...] = total
        fetch("ok", gain_buf, out_gain)

    def f4g(b):
        rg[4](b)
        for first in range(0, RB, 16):
            grad_in = rg[5](b, first, 16)
            r = pl.ds(pl.multiple_of(b * M + j * RB + first, 16), 16)
            scale = inv[r, :]
            normed = tok[r, :].astype(F32) * scale
            grad_normed = grad_in * gain_row
            mean = jnp.mean(grad_normed * normed, axis=-1, keepdims=True)
            outt[pl.ds(b * RB + first, 16), :] = (
                go[r, :].astype(F32) + scale * (grad_normed - normed * mean)
            ).astype(BF16)
        fetch(("ot", b), outt.at[pl.ds(b * RB, RB)], out_tokens.at[0, pl.ds(b * RB, RB)])

    def weight(name, left, right, dst, out, size):
        def task(i):
            r = pl.ds(i * size, size)
            dst[r, :] = dot_tn(left[:, i * size : (i + 1) * size], right[...]).astype(BF16)
            fetch((name, i), dst.at[r], out.at[0, r])

        return task

    def n1(b):
        onward(b, "o")

    tasks = {
        "N": n1,
        "P1": p1, "P2": p2, "P3": p3, "P4": p4, "O1": o1, "O2": o2, "O3": o3, "F0": f0, "F4": f4,
        "F2": ra[1], "F2b": ra[2], "F3": ra[3], "S2": rg[1], "S2b": rg[2], "S3": rg[3], "S4": f4g,
        "B1": b1, "B2": b2, "B3": b3, "B4": b4, "K1": k1, "K2": k2,
        "WD": weight("wd", hid, go, sd, out_down, 256),
        "WG": weight("wg", x, ggp, sg, out_gate, 256),
        "WU": weight("wu", x, gup, su, out_up, 256),
    }
    for i in range(7):
        tasks["E%d" % (i + 1)] = ea[i]
        tasks["G%d" % (i + 1)] = eg[i]
    for name, index in ORDER:
        tasks[name](index)

    for key, copy in sent:
        if key not in waited:
            copy.wait_send()
    for key in locals_:
        need(key)


def hand_over(*refs):
    sources, results, holds, sems = refs[:5], refs[5:10], refs[10:15], refs[15]
    steps = []
    for i, (src, hold, dst) in enumerate(zip(sources, holds, results)):
        whole = src.shape[1]
        parts = 4 if 0 < i < 4 else 1
        for part in range(parts):
            r = pl.ds(part * (whole // parts), whole // parts)
            steps.append((
                pltpu.make_async_copy(src.at[:, r], hold.at[:, r], sems.at[0, i, part]),
                pltpu.make_async_copy(hold.at[:, r], dst.at[:, r], sems.at[1, i, part]),
            ))
    for first, _ in steps:
        first.start()
    for first, second in steps:
        first.wait()
        second.start()
    for _, second in steps:
        second.wait()


def shards(
    tokens, upstream, gate_weight, up_weight, down_weight, norm_gain,
    stale_gate, stale_up, stale_down, stale_gain,
):
    hbm = pl.BlockSpec(memory_space=pl.ANY)
    vmem = pl.BlockSpec(memory_space=pltpu.VMEM)
    total = N * ROWS
    wide = pltpu.VMEM((total, D), BF16)
    narrow = pltpu.VMEM((total, FB), F32)
    half = pltpu.VMEM((total, FB), BF16)
    tall = pltpu.VMEM((D, FB), BF16)
    flat = pltpu.VMEM((FB, D), BF16)
    step = pltpu.VMEM((M, FB), F32)
    land = pltpu.VMEM((NB * 7 * RB, D), BF16)
    results = (
        jax.ShapeDtypeStruct((1, ROWS, D), BF16),
        jax.ShapeDtypeStruct((1, D, FB), BF16),
        jax.ShapeDtypeStruct((1, D, FB), BF16),
        jax.ShapeDtypeStruct((1, FB, D), BF16),
        jax.ShapeDtypeStruct((1, D), F32),
    )
    parts = pl.pallas_call(
        kernel,
        out_shape=results,
        in_specs=[hbm, hbm, hbm, hbm, hbm, vmem, hbm, hbm, hbm, vmem],
        out_specs=(hbm,) * 5,
        scratch_shapes=[
            tall, tall, flat, tall, tall, flat,
            pltpu.VMEM((ROWS, D), BF16),
            wide, wide, wide,
            pltpu.VMEM((M, D), BF16),
            pltpu.VMEM((total, 1), F32),
            narrow, narrow, step, step, half,
            pltpu.VMEM((M, FB), BF16),
            wide, wide, land, land, wide, half, half,
            pltpu.VMEM((ROWS, D), BF16),
            pltpu.VMEM((8, D), F32),
            pltpu.VMEM((1, D), F32),
            pltpu.VMEM((N, 1, D), F32),
            pltpu.VMEM((1, D), F32),
            pltpu.SemaphoreType.DMA((NB * 38 + 8,)),
            pltpu.SemaphoreType.DMA((NB * 38 + 8,)),
            pltpu.SemaphoreType.DMA((2 * NB + 7 + 16,)),
        ],
        compiler_params=pltpu.CompilerParams(
            collective_id=0, has_side_effects=True, vmem_limit_bytes=62 * 2**20
        ),
        name="layer",
    )(
        tokens, upstream, gate_weight, up_weight, down_weight, norm_gain,
        stale_gate, stale_up, stale_down, stale_gain,
    )
    return pl.pallas_call(
        hand_over,
        out_shape=results,
        in_specs=[hbm] * 5,
        out_specs=(hbm,) * 5,
        scratch_shapes=[pltpu.VMEM(r.shape, r.dtype) for r in results]
        + [pltpu.SemaphoreType.DMA((2, 5, 4))],
        compiler_params=pltpu.CompilerParams(vmem_limit_bytes=62 * 2**20),
        name="hand_over",
    )(*parts)


def solution(mesh):
    in_specs = (
        P("member", "fsdp", None),
        P("member", "fsdp", None),
        P("member", None, "fsdp"),
        P("member", None, "fsdp"),
        P("member", "fsdp", None),
        P("member", None),
        P("member", None, "fsdp"),
        P("member", None, "fsdp"),
        P("member", "fsdp", None),
        P("member", None),
    )
    out_specs = (
        P("member", "fsdp", None),
        P("member", None, "fsdp"),
        P("member", None, "fsdp"),
        P("member", "fsdp", None),
        P("member", None),
    )
    return jax.shard_map(shards, mesh=mesh, in_specs=in_specs, out_specs=out_specs, check_vma=False)
```

```python
import functools
import jax
import jax.numpy as jnp
from jax import lax
from jax.experimental import pallas as pl
from jax.experimental.pallas import tpu as pltpu
from jax.sharding import PartitionSpec as P

EPS = 1e-05
AGREE = 1.0
MESH = pl.DeviceIdType.MESH
F32 = jnp.float32
BF16 = jnp.bfloat16
D = 1536
FB = 768
N = 8
ROWS = 128
NB = 4
RB = ROWS // NB
KR, KG, KS = 1, 2, 2
M = N * RB

ORDER = [('E1', 0), ('E1', 2), ('E3', 0), ('E2', 0), ('E1', 1), ('E5', 0), ('E6', 0), ('E3', 1), ('E4', 0), ('E2', 1), ('E7', 0), ('O1', 0), ('E5', 1), ('E6', 1), ('E3', 2), ('E4', 1), ('E1', 3), ('N', 1), ('E3', 3), ('P1', 0), ('P2', 0), ('P4', 0), ('E7', 1), ('N', 2), ('E2', 2), ('E5', 2), ('E4', 2), ('E6', 2), ('O1', 1), ('O2', 0), ('P1', 1), ('P2', 1), ('E2', 3), ('P4', 1), ('E7', 2), ('E5', 3), ('E4', 3), ('N', 3), ('E6', 3), ('O2', 1), ('F0', 0), ('P1', 2), ('P2', 2), ('P4', 2), ('E7', 3), ('F2', 0), ('F0', 1), ('O1', 2), ('O2', 2), ('F2b', 0), ('F3', 0), ('F2', 1), ('P1', 3), ('P2', 3), ('F0', 2), ('P4', 3), ('F2', 2), ('F4', 0), ('O1', 3), ('F2b', 2), ('F2b', 1), ('O2', 3), ('F3', 2), ('F3', 1), ('F0', 3), ('F2', 3), ('G2', 0), ('G5', 0), ('F4', 2), ('F2b', 3), ('F4', 1), ('G3', 0), ('F3', 3), ('G2', 1), ('G4', 0), ('G3', 2), ('G3', 1), ('G6', 0), ('G2', 2), ('F4', 3), ('G7', 0), ('G5', 2), ('G4', 1), ('G5', 1), ('G6', 2), ('B1', 0), ('G2', 3), ('G4', 2), ('B2', 0), ('G6', 1), ('G7', 1), ('G4', 3), ('B1', 1), ('G3', 3), ('S2', 0), ('G7', 2), ('B2', 1), ('G5', 3), ('B1', 2), ('S2b', 0), ('B2', 2), ('G7', 3), ('S2b', 1), ('G6', 3), ('B1', 3), ('S2', 1), ('S3', 0), ('WD', 1), ('B2', 3), ('S2', 2), ('B4', 3), ('S2b', 2), ('WU', 0), ('WU', 1), ('S2', 3), ('S3', 1), ('S3', 2), ('WU', 2), ('S2b', 3), ('WD', 2), ('S4', 0), ('WU', 3), ('S4', 1), ('S3', 3), ('WD', 0), ('S4', 2), ('K1', 0), ('WU', 4), ('WU', 5), ('S4', 3), ('K2', 0)]


def dot_nn(a, b):
    return jnp.dot(a, b, preferred_element_type=F32)


def dot_nt(a, b):
    return lax.dot_general(a, b, (((1,), (1,)), ((), ())), preferred_element_type=F32)


def dot_tn(a, b):
    return lax.dot_general(a, b, (((0,), (0,)), ((), ())), preferred_element_type=F32)


def blocks(total, size, body):
    @pl.loop(0, total // size)
    def _(i):
        body(pl.multiple_of(i * size, size))


def kernel(
    tokens, upstream, gate_w, up_w, down_w, gain, stale_gate, stale_up, stale_down, stale_gain,
    out_tokens, out_gate, out_up, out_down, out_gain,
    wgu, wd, sgu, sd, ups, tok, tok_next, x, xs, inv, guv, gut, hid, hid_s,
    gap, peer, rs1, rs2, go, gp, outt, acc, acc_out, acc_in, gain_buf,
    send, recv, local,
):
    member = lax.axis_index("member")
    j = lax.axis_index("fsdp")
    y, z = j // 4, j % 4
    members = lax.axis_size("member")
    z_up, z_dn, z_far = (z + 1) % 4, (z + 3) % 4, (z + 2) % 4
    other = 1 - y
    UP, DN, ACROSS = (member, y * 4 + z_up), (member, y * 4 + z_dn), (member, other * 4 + z)
    NEXT = ((member + 1) % members, j)
    PREV = ((member + members - 1) % members, j)
    edge_prev, edge_next = ((member + 7) % 8) // 7, (member % 8) // 7
    PREV_X = (PREV[0], ((y + edge_prev) % 2) * 4 + z)
    NEXT_X = (NEXT[0], ((y + edge_next) % 2) * 4 + z)

    pos = {
        "o": j,
        "ou": y * 4 + z_up,
        "od": y * 4 + z_dn,
        "of": y * 4 + z_far,
        "x": other * 4 + z,
        "xu": other * 4 + z_up,
        "xd": other * 4 + z_dn,
        "xf": other * 4 + z_far,
    }

    def rows(b, chunk):
        return pl.ds(pl.multiple_of(b * M + pos[chunk] * RB, 16), RB)

    def batch(b):
        return pl.ds(b * M, M)

    numbers = {}

    def number(key):
        return numbers.setdefault(key, len(numbers))

    def remote(key, src, dst, device):
        i = number(key)
        return pltpu.make_async_remote_copy(
            src_ref=src,
            dst_ref=dst,
            send_sem=send.at[i],
            recv_sem=recv.at[i],
            device_id=device,
            device_id_type=MESH,
        )

    sent = []

    def start(key, src, dst, device):
        copy = remote(key, src, dst, device)
        copy.start()
        sent.append((key, copy))

    def arrive(key, dst, device):
        remote(key, dst, dst, device).wait_recv()

    locals_ = {}

    def fetch(key, src, dst):
        copy = pltpu.make_async_copy(src, dst, local.at[len(locals_)])
        locals_[key] = copy
        copy.start()

    done = set()

    def need(key):
        if key not in done:
            done.add(key)
            locals_[key].wait()

    barrier = pltpu.get_barrier_semaphore()
    for step in range(1, N):
        pl.semaphore_signal(barrier, inc=1, device_id=(member, (j + step) % N), device_id_type=MESH)
    for to in (NEXT[0], PREV[0]):
        for at in (y, other):
            pl.semaphore_signal(barrier, inc=1, device_id=(to, at * 4 + z), device_id_type=MESH)
    for b in range(NB):
        fetch(("t", b), tokens.at[0, pl.ds(b * RB, RB)], tok.at[rows(b, "o")])
    left, right = pl.ds(0, FB), pl.ds(FB, FB)
    fetch("sg", stale_gate.at[0], sgu.at[:, left])
    fetch("su", stale_up.at[0], sgu.at[:, right])
    fetch("sd", stale_down.at[0], sd)
    fetch("wg", gate_w.at[0], wgu.at[:, left])
    fetch("wu", up_w.at[0], wgu.at[:, right])
    fetch("wd", down_w.at[0], wd)
    fetch("ups", upstream.at[0], ups)
    acc[...] = jnp.zeros_like(acc)
    pl.semaphore_wait(barrier, N + 3)

    mirror = {"ou": "od", "od": "ou", "xu": "xd", "xd": "xu"}

    def side(b, chunk):
        return mirror.get(chunk, chunk) if b % 2 else chunk

    def ways(b):
        return (DN, UP) if b % 2 else (UP, DN)

    def onward(b, chunk):
        chunk = side(b, chunk)
        if chunk[0] == "o":
            start(("n", b, chunk), tok.at[rows(b, chunk)], tok_next.at[rows(b, chunk)], PREV)
        else:
            at = ((other + edge_prev) % 2) * 4 + pos[chunk] % 4
            r = pl.ds(pl.multiple_of(b * M + at * RB, 16), RB)
            start(("n", b, chunk), tok.at[r], tok_next.at[r], PREV_X)

    def gather(name, ref, then, crossings):
        def move(b, chunk, way, device):
            r = rows(b, side(b, chunk))
            start((name, b, chunk, way), ref.at[r], ref.at[r], device)

        def got(b, chunk, sent_as, way):
            arrive((name, b, sent_as, way), ref.at[rows(b, side(b, chunk))], UP)

        def e1(b):
            up, dn = ways(b)
            if name == "g":
                move(b, "o", "a", ACROSS)
            elif b == 0:
                for each in range(NB):
                    need(("t", each))
                    move(each, "o", "a", ACROSS)
                    if each == 0:
                        move(b, "o", "u", up)
                        move(b, "o", "d", dn)
                then(b, "o")
                return
            move(b, "o", "u", up)
            move(b, "o", "d", dn)

        def e2(b):
            got(b, "od", "o", "u")
            if crossings == 2:
                move(b, "od", "a", ACROSS)
            move(b, "od", "u", ways(b)[0])
            then(b, "od")

        def e3(b):
            got(b, "x", "o", "a")
            move(b, "x", "d", ways(b)[1])
            if crossings == 1:
                move(b, "x", "u", ways(b)[0])
            then(b, "x")

        def e4(b):
            if crossings == 2:
                got(b, "xd", "od", "a")
                move(b, "xd", "u", ways(b)[0])
            else:
                got(b, "xd", "x", "u")
            then(b, "xd")

        def e5(b):
            got(b, "ou", "o", "d")
            then(b, "ou")

        def e6(b):
            got(b, "xu", "x", "d")
            if crossings == 1:
                move(b, "xu", "d", ways(b)[1])
            then(b, "xu")

        def e7(b):
            got(b, "of", "od", "u")
            if crossings == 2:
                got(b, "xf", "xd", "u")
            else:
                got(b, "xf", "xu", "d")
            then(b, "of")
            then(b, "xf")

        return e1, e2, e3, e4, e5, e6, e7

    def scatter(name, ref, land, crossings):
        def slot(b, k):
            return land.at[pl.ds((b * 7 + k) * RB, RB)]

        def push(b, chunk, k, device):
            start((name, b, k), ref.at[rows(b, side(b, chunk))], slot(b, k), device)

        def merge(b, chunk, slots, k, device):
            for each in slots:
                arrive((name, b, each), slot(b, each), UP)
            total = ref[rows(b, side(b, chunk)), :].astype(F32)
            for each in slots:
                total = total + slot(b, each)[...].astype(F32)
            at = slot(b, slots[0])
            at[...] = total.astype(BF16)
            start((name, b, k), at, slot(b, k), device)

        last = (3, 5, 6) if crossings == 2 else (2, 5, 6)

        def f1(b):
            up, dn = ways(b)
            if crossings == 2:
                push(b, "xf", 0, dn)
                push(b, "xu", 2, up)
                push(b, "of", 1, dn)
                push(b, "ou", 3, up)
            else:
                push(b, "xf", 0, up)
                push(b, "xd", 3, dn)
                push(b, "of", 1, dn)
                push(b, "ou", 2, up)

        def f2(b):
            if crossings == 2:
                merge(b, "xd", (0,), 4, ACROSS)
            else:
                merge(b, "xu", (0,), 4, ways(b)[0])

        def f2b(b):
            if crossings == 2:
                merge(b, "x", (2,), 5, ACROSS)
            else:
                merge(b, "od", (1,), 5, ways(b)[1])

        def f3(b):
            if crossings == 2:
                merge(b, "od", (1, 4), 6, ways(b)[1])
            else:
                merge(b, "x", (3, 4), 6, ACROSS)

        def f4(b):
            for k in last:
                arrive((name, b, k), slot(b, k), UP)

        def result(b, first, size):
            at = pl.multiple_of(b * M + j * RB + first, 16)
            total = ref[pl.ds(at, size), :].astype(F32)
            for k in last:
                total = total + land[pl.ds((b * 7 + k) * RB + first, size), :].astype(F32)
            return total

        return f1, f2, f2b, f3, f4, result

    ea = gather("a", tok, onward, 1)
    eg = gather("g", go, lambda b, chunk: None, KG)
    ra = scatter("r", gap, rs1, KR)
    rg = scatter("s", peer, rs2, KS)

    gain_row = gain[...].astype(F32)
    stale_row = stale_gain[...].astype(F32)

    def normalize(src, dst, at_dst, b, factor, keep):
        def body(at):
            values = src[pl.ds(pl.multiple_of(b * M + at, 16), 16), :].astype(F32)
            scale = lax.rsqrt(jnp.mean(values * values, axis=-1, keepdims=True) + EPS)
            dst[pl.ds(pl.multiple_of(at_dst + at, 16), 16), :] = (values * scale * factor).astype(BF16)
            if keep:
                inv[pl.ds(pl.multiple_of(b * M + at, 16), 16), :] = scale

        blocks(M, 16, body)

    def activate(ref, base, dst, at_dst):
        def body(at):
            r = pl.ds(pl.multiple_of(base + at, 16), 16)
            g, u = ref[r, left], ref[r, right]
            dst[pl.ds(pl.multiple_of(at_dst + at, 16), 16), :] = (g * jax.nn.sigmoid(g) * u).astype(BF16)

        blocks(M, 16, body)

    def p1(b):
        for chunk in pos:
            arrive(("n", b, chunk), tok_next.at[rows(b, chunk)], PREV)
        normalize(tok_next, xs, 0, b, stale_row, False)

    def p2(b):
        need("sg")
        need("su")
        gut[...] = dot_nn(xs[...], sgu[...])
        activate(gut, 0, hid_s, 0)

    def p4(b):
        need("sd")
        peer[batch(b), :] = dot_nn(hid_s[...], sd[...]).astype(BF16)
        for half, device in ((0, NEXT), (1, NEXT_X)):
            r = pl.ds(b * M + half * (M // 2), M // 2)
            start(("p", b, half), peer.at[r], gap.at[r], device)

    def o1(b):
        normalize(tok, x, b * M, b, gain_row, True)

    def o2(b):
        need("wg")
        need("wu")
        guv[batch(b), :] = dot_nn(x[batch(b), :], wgu[...])
        activate(guv, b * M, hid, b * M)

    def f0(b):
        need("wd")
        for half in range(2):
            arrive(("p", b, half), gap.at[pl.ds(b * M + half * (M // 2), M // 2)], PREV)
        own = dot_nn(hid[batch(b), :], wd[...])
        gap[batch(b), :] = (own - gap[batch(b), :].astype(F32)).astype(BF16)
        ra[0](b)

    def f4(b):
        need("ups")
        ra[4](b)
        for first in range(0, RB, 16):
            total = ra[5](b, first, 16)
            mine = ups[pl.ds(b * RB + first, 16), :].astype(F32) + AGREE * total
            go[pl.ds(pl.multiple_of(b * M + j * RB + first, 16), 16), :] = mine.astype(BF16)
        eg[0](b)

    def b1(b):
        gut[:, left] = dot_nt(go[batch(b), :], wd[...])

        def body(at):
            r = pl.ds(pl.multiple_of(b * M + at, 16), 16)
            g, u = guv[r, left], guv[r, right]
            s = jax.nn.sigmoid(g)
            gh = gut[pl.ds(at, 16), left]
            gp[r, left] = (gh * u * s * (1.0 + g * (1.0 - s))).astype(BF16)
            gp[r, right] = (gh * (g * s)).astype(BF16)

        blocks(M, 16, body)

    waited = set()

    def b2(b):
        for key, copy in sent:
            if key[:2] == ("p", b):
                copy.wait_send()
                waited.add(key)
        peer[batch(b), :] = dot_nt(gp[batch(b), :], wgu[...]).astype(BF16)
        rg[0](b)

    def b4(b):
        def body(at):
            r = pl.ds(pl.multiple_of(b * M + at, 16), 16)
            part = peer[r, :].astype(F32) * (tok[r, :].astype(F32) * inv[r, :])
            acc[...] += part[:8] + part[8:]

        blocks(M, 16, body)

    def k1(b):
        acc_out[...] = jnp.sum(acc[...], axis=0, keepdims=True)
        for step in range(1, N):
            start(("k", step), acc_out, acc_in.at[step], (member, (j + step) % N))

    def k2(b):
        total = acc_out[...]
        for step in range(1, N):
            arrive(("k", step), acc_in.at[step], (member, (j + step) % N))
            total = total + acc_in[step]
        gain_buf[...] = total
        fetch("ok", gain_buf, out_gain)

    def f4g(b):
        rg[4](b)
        for first in range(0, RB, 16):
            grad_in = rg[5](b, first, 16)
            r = pl.ds(pl.multiple_of(b * M + j * RB + first, 16), 16)
            scale = inv[r, :]
            normed = tok[r, :].astype(F32) * scale
            grad_normed = grad_in * gain_row
            mean = jnp.mean(grad_normed * normed, axis=-1, keepdims=True)
            if b < NB - 1:
                part = grad_in * normed
                acc[...] += part[:8] + part[8:]
            outt[pl.ds(b * RB + first, 16), :] = (
                go[r, :].astype(F32) + scale * (grad_normed - normed * mean)
            ).astype(BF16)
        fetch(("ot", b), outt.at[pl.ds(b * RB, RB)], out_tokens.at[0, pl.ds(b * RB, RB)])

    def weight_down(i):
        r = pl.ds(i * 256, 256)
        sd[r, :] = dot_tn(hid[:, i * 256 : (i + 1) * 256], go[...]).astype(BF16)
        fetch(("d", i), sd.at[r], out_down.at[0, r])

    def weight_up(i):
        r = pl.ds(i * 256, 256)
        sgu[r, :] = dot_tn(x[:, i * 256 : (i + 1) * 256], gp[...]).astype(BF16)
        fetch(("g", i), sgu.at[r, left], out_gate.at[0, r])
        fetch(("u", i), sgu.at[r, right], out_up.at[0, r])

    def n1(b):
        onward(b, "o")

    tasks = {
        "N": n1,
        "P1": p1, "P2": p2, "P4": p4, "O1": o1, "O2": o2, "F0": f0, "F4": f4,
        "F2": ra[1], "F2b": ra[2], "F3": ra[3], "S2": rg[1], "S2b": rg[2], "S3": rg[3], "S4": f4g,
        "B1": b1, "B2": b2, "B4": b4, "K1": k1, "K2": k2, "WD": weight_down, "WU": weight_up,
    }
    for i in range(7):
        tasks["E%d" % (i + 1)] = ea[i]
        tasks["G%d" % (i + 1)] = eg[i]
    for name, index in ORDER:
        tasks[name](index)

    for key, copy in sent:
        if key not in waited:
            copy.wait_send()
    for key in locals_:
        need(key)


def hand_over(*refs):
    sources, results, holds, sems = refs[:5], refs[5:10], refs[10:15], refs[15]
    steps = []
    for i, (src, hold, dst) in enumerate(zip(sources, holds, results)):
        whole = src.shape[1]
        parts = 4 if 0 < i < 4 else 1
        for part in range(parts):
            r = pl.ds(part * (whole // parts), whole // parts)
            steps.append((
                pltpu.make_async_copy(src.at[:, r], hold.at[:, r], sems.at[0, i, part]),
                pltpu.make_async_copy(hold.at[:, r], dst.at[:, r], sems.at[1, i, part]),
            ))
    for first, _ in steps:
        first.start()
    for first, second in steps:
        first.wait()
        second.start()
    for _, second in steps:
        second.wait()


def shards(
    tokens, upstream, gate_weight, up_weight, down_weight, norm_gain,
    stale_gate, stale_up, stale_down, stale_gain,
):
    hbm = pl.BlockSpec(memory_space=pl.ANY)
    vmem = pl.BlockSpec(memory_space=pltpu.VMEM)
    total = N * ROWS
    wide = pltpu.VMEM((total, D), BF16)
    half = pltpu.VMEM((total, FB), BF16)
    square = pltpu.VMEM((D, D), BF16)
    flat = pltpu.VMEM((FB, D), BF16)
    land = pltpu.VMEM((NB * 7 * RB, D), BF16)
    results = (
        jax.ShapeDtypeStruct((1, ROWS, D), BF16),
        jax.ShapeDtypeStruct((1, D, FB), BF16),
        jax.ShapeDtypeStruct((1, D, FB), BF16),
        jax.ShapeDtypeStruct((1, FB, D), BF16),
        jax.ShapeDtypeStruct((1, D), F32),
    )
    parts = pl.pallas_call(
        kernel,
        out_shape=results,
        in_specs=[hbm, hbm, hbm, hbm, hbm, vmem, hbm, hbm, hbm, vmem],
        out_specs=(hbm,) * 5,
        scratch_shapes=[
            square, flat, square, flat,
            pltpu.VMEM((ROWS, D), BF16),
            wide, wide, wide,
            pltpu.VMEM((M, D), BF16),
            pltpu.VMEM((total, 1), F32),
            pltpu.VMEM((total, D), F32), pltpu.VMEM((M, D), F32), half,
            pltpu.VMEM((M, FB), BF16),
            wide, wide, land, land, wide, wide,
            pltpu.VMEM((ROWS, D), BF16),
            pltpu.VMEM((8, D), F32),
            pltpu.VMEM((1, D), F32),
            pltpu.VMEM((N, 1, D), F32),
            pltpu.VMEM((1, D), F32),
            pltpu.SemaphoreType.DMA((NB * 38 + 8,)),
            pltpu.SemaphoreType.DMA((NB * 38 + 8,)),
            pltpu.SemaphoreType.DMA((2 * NB + 7 + 16,)),
        ],
        compiler_params=pltpu.CompilerParams(
            collective_id=0, has_side_effects=True, vmem_limit_bytes=62 * 2**20
        ),
        name="layer",
    )(
        tokens, upstream, gate_weight, up_weight, down_weight, norm_gain,
        stale_gate, stale_up, stale_down, stale_gain,
    )
    return pl.pallas_call(
        hand_over,
        out_shape=results,
        in_specs=[hbm] * 5,
        out_specs=(hbm,) * 5,
        scratch_shapes=[pltpu.VMEM(r.shape, r.dtype) for r in results]
        + [pltpu.SemaphoreType.DMA((2, 5, 4))],
        compiler_params=pltpu.CompilerParams(vmem_limit_bytes=62 * 2**20),
        name="hand_over",
    )(*parts)


def solution(mesh):
    in_specs = (
        P("member", "fsdp", None),
        P("member", "fsdp", None),
        P("member", None, "fsdp"),
        P("member", None, "fsdp"),
        P("member", "fsdp", None),
        P("member", None),
        P("member", None, "fsdp"),
        P("member", None, "fsdp"),
        P("member", "fsdp", None),
        P("member", None),
    )
    out_specs = (
        P("member", "fsdp", None),
        P("member", None, "fsdp"),
        P("member", None, "fsdp"),
        P("member", "fsdp", None),
        P("member", None),
    )
    return jax.shard_map(shards, mesh=mesh, in_specs=in_specs, out_specs=out_specs, check_vma=False)
```

```python
import functools
import jax
import jax.numpy as jnp
from jax import lax
from jax.experimental import pallas as pl
from jax.experimental.pallas import tpu as pltpu
from jax.sharding import PartitionSpec as P

EPS = 1e-05
AGREE = 1.0
MESH = pl.DeviceIdType.MESH
F32 = jnp.float32
BF16 = jnp.bfloat16
D = 1536
FB = 768
N = 8
ROWS = 128
RB = (16, 16, 32, 32, 32)
NB = len(RB)
FIRST = tuple(sum(RB[:b]) for b in range(NB))
CROSS = {"a": (1,) * 5, "r": (1, 1, 1, 1, 2), "g": (1, 1, 2, 2, 2), "s": (2,) * 5}
M = tuple(N * size for size in RB)
BASE = tuple(N * first for first in FIRST)

ORDER = (
    ("E1", 0), ("N", 1), ("E1", 2), ("N", 2), ("E1", 1), ("E5", 0), ("E3", 0), ("E3", 1), ("E5", 2),
    ("E2", 1), ("E5", 1), ("E2", 0), ("E6", 0), ("E4", 0), ("E3", 2), ("E1", 3), ("E7", 0), ("E6", 1),
    ("O1", 0), ("O2", 0), ("E6", 2), ("E2", 2), ("P1", 0), ("E1", 4), ("E4", 1), ("E7", 1), ("P2", 0),
    ("P4", 0), ("E4", 2), ("E7", 2), ("E3", 3), ("O1", 1), ("E5", 3), ("E2", 3), ("P1", 1), ("P2", 1),
    ("P4", 1), ("E6", 3), ("E4", 3), ("E3", 4), ("E2", 4), ("P1", 2), ("P2", 2), ("E7", 3), ("P4", 2),
    ("N", 3), ("E5", 4), ("N", 4), ("F0", 0), ("O2", 1), ("F0", 1), ("E6", 4), ("O1", 2), ("F2", 1),
    ("F2", 0), ("F2b", 0), ("E4", 4), ("P1", 3), ("P2", 3), ("P4", 3), ("E7", 4), ("F3", 1), ("F2b", 1),
    ("F3", 0), ("O2", 2), ("F0", 2), ("O1", 3), ("P1", 4), ("F2", 2), ("P2", 4), ("F2b", 2), ("F4", 1),
    ("O2", 3), ("F4", 0), ("F3", 2), ("F0", 3), ("P4", 4), ("O1", 4), ("G3", 1), ("O2", 4), ("F4", 2),
    ("G3", 0), ("G5", 1), ("F2", 3), ("G2", 1), ("G2", 0), ("G2", 2), ("F2b", 3), ("G5", 0), ("G6", 0),
    ("G6", 1), ("G4", 1), ("F0", 4), ("G7", 0), ("G4", 0), ("F3", 3), ("B1", 0), ("G3", 2), ("B2", 0),
    ("G7", 1), ("F2", 4), ("F2b", 4), ("B1", 1), ("F4", 3), ("G4", 2), ("F3", 4), ("G5", 2), ("S2", 0),
    ("B2", 1), ("G2", 3), ("S2b", 0), ("G6", 2), ("G3", 3), ("G7", 2), ("B1", 2), ("F4", 4), ("G4", 3),
    ("B2", 2), ("G5", 4), ("G3", 4), ("G2", 4), ("S2", 1), ("S3", 0), ("G5", 3), ("S2b", 1), ("G6", 3),
    ("G7", 3), ("S2b", 2), ("B1", 3), ("G4", 4), ("S2", 2), ("B2", 3), ("S3", 1), ("G6", 4), ("G7", 4),
    ("B1", 4), ("B2", 4), ("S2", 3), ("S2b", 3), ("WD", 2), ("S3", 2), ("B4", 4), ("S4", 1), ("WU", 4),
    ("S2", 4), ("S3", 3), ("WD", 0), ("WU", 2), ("S2b", 4), ("WD", 1), ("S4", 0), ("S4", 2), ("S4", 3),
    ("S3", 4), ("K1", 0), ("WU", 3), ("WU", 0), ("WU", 5), ("WU", 1), ("S4", 4), ("K2", 0),
)


def dot_nn(a, b):
    return jnp.dot(a, b, preferred_element_type=F32)


def dot_nt(a, b):
    return lax.dot_general(a, b, (((1,), (1,)), ((), ())), preferred_element_type=F32)


def dot_tn(a, b):
    return lax.dot_general(a, b, (((0,), (0,)), ((), ())), preferred_element_type=F32)


def blocks(total, size, body):
    @pl.loop(0, total // size)
    def _(i):
        body(pl.multiple_of(i * size, size))


def kernel(
    tokens, upstream, gate_w, up_w, down_w, gain, stale_gate, stale_up, stale_down, stale_gain,
    out_tokens, out_gate, out_up, out_down, out_gain,
    wgu, wd, sgu, sd, ups, tok, tok_next, x, xs, inv, guv, gut, hid, hid_s,
    gap, peer, rs1, rs2, go, gp, outt, acc, acc_out, acc_in, gain_buf,
    send, recv, local,
):
    member = lax.axis_index("member")
    j = lax.axis_index("fsdp")
    y, z = j // 4, j % 4
    members = lax.axis_size("member")
    z_up, z_dn, z_far = (z + 1) % 4, (z + 3) % 4, (z + 2) % 4
    other = 1 - y
    UP, DN, ACROSS = (member, y * 4 + z_up), (member, y * 4 + z_dn), (member, other * 4 + z)
    NEXT = ((member + 1) % members, j)
    PREV = ((member + members - 1) % members, j)
    edge_prev, edge_next = ((member + 7) % 8) // 7, (member % 8) // 7
    PREV_X = (PREV[0], ((y + edge_prev) % 2) * 4 + z)
    NEXT_X = (NEXT[0], ((y + edge_next) % 2) * 4 + z)

    pos = {
        "o": j,
        "ou": y * 4 + z_up,
        "od": y * 4 + z_dn,
        "of": y * 4 + z_far,
        "x": other * 4 + z,
        "xu": other * 4 + z_up,
        "xd": other * 4 + z_dn,
        "xf": other * 4 + z_far,
    }

    def rows(b, chunk):
        return pl.ds(pl.multiple_of(BASE[b] + pos[chunk] * RB[b], 16), RB[b])

    def batch(b):
        return pl.ds(BASE[b], M[b])

    numbers = {}

    def number(key):
        return numbers.setdefault(key, len(numbers))

    def remote(key, src, dst, device):
        i = number(key)
        return pltpu.make_async_remote_copy(
            src_ref=src,
            dst_ref=dst,
            send_sem=send.at[i],
            recv_sem=recv.at[i],
            device_id=device,
            device_id_type=MESH,
        )

    sent = []

    def start(key, src, dst, device):
        copy = remote(key, src, dst, device)
        copy.start()
        sent.append((key, copy))

    def arrive(key, dst, device):
        remote(key, dst, dst, device).wait_recv()

    locals_ = {}

    def fetch(key, src, dst):
        copy = pltpu.make_async_copy(src, dst, local.at[len(locals_)])
        locals_[key] = copy
        copy.start()

    done = set()

    def need(key):
        if key not in done:
            done.add(key)
            locals_[key].wait()

    barrier = pltpu.get_barrier_semaphore()
    for step in range(1, N):
        pl.semaphore_signal(barrier, inc=1, device_id=(member, (j + step) % N), device_id_type=MESH)
    for to in (NEXT[0], PREV[0]):
        for at in (y, other):
            pl.semaphore_signal(barrier, inc=1, device_id=(to, at * 4 + z), device_id_type=MESH)
    for b in range(NB):
        fetch(("t", b), tokens.at[0, pl.ds(FIRST[b], RB[b])], tok.at[rows(b, "o")])
    left, right = pl.ds(0, FB), pl.ds(FB, FB)
    fetch("sg", stale_gate.at[0], sgu.at[:, left])
    fetch("su", stale_up.at[0], sgu.at[:, right])
    fetch("sd", stale_down.at[0], sd)
    fetch("wg", gate_w.at[0], wgu.at[:, left])
    fetch("wu", up_w.at[0], wgu.at[:, right])
    fetch("wd", down_w.at[0], wd)
    fetch("ups", upstream.at[0], ups)
    acc[...] = jnp.zeros_like(acc)
    pl.semaphore_wait(barrier, N + 3)

    mirror = {"ou": "od", "od": "ou", "xu": "xd", "xd": "xu"}

    def side(b, chunk):
        return mirror.get(chunk, chunk) if b % 2 else chunk

    def ways(b):
        return (DN, UP) if b % 2 else (UP, DN)

    def onward(b, chunk):
        chunk = side(b, chunk)
        if chunk[0] == "o":
            start(("n", b, chunk), tok.at[rows(b, chunk)], tok_next.at[rows(b, chunk)], PREV)
        else:
            at = ((other + edge_prev) % 2) * 4 + pos[chunk] % 4
            r = pl.ds(pl.multiple_of(BASE[b] + at * RB[b], 16), RB[b])
            start(("n", b, chunk), tok.at[r], tok_next.at[r], PREV_X)

    def gather(name, ref, then, crossings):
        def move(b, chunk, way, device):
            r = rows(b, side(b, chunk))
            start((name, b, chunk, way), ref.at[r], ref.at[r], device)

        def got(b, chunk, sent_as, way):
            arrive((name, b, sent_as, way), ref.at[rows(b, side(b, chunk))], UP)

        def e1(b):
            up, dn = ways(b)
            if name == "g":
                move(b, "o", "a", ACROSS)
            elif b == 0:
                for each in range(NB):
                    need(("t", each))
                    move(each, "o", "a", ACROSS)
                    if each == 0:
                        move(b, "o", "u", up)
                        move(b, "o", "d", dn)
                then(b, "o")
                return
            move(b, "o", "u", up)
            move(b, "o", "d", dn)

        def e2(b):
            got(b, "od", "o", "u")
            if crossings[b] == 2:
                move(b, "od", "a", ACROSS)
            move(b, "od", "u", ways(b)[0])
            then(b, "od")

        def e3(b):
            got(b, "x", "o", "a")
            move(b, "x", "d", ways(b)[1])
            if crossings[b] == 1:
                move(b, "x", "u", ways(b)[0])
            then(b, "x")

        def e4(b):
            if crossings[b] == 2:
                got(b, "xd", "od", "a")
                move(b, "xd", "u", ways(b)[0])
            else:
                got(b, "xd", "x", "u")
            then(b, "xd")

        def e5(b):
            got(b, "ou", "o", "d")
            then(b, "ou")

        def e6(b):
            got(b, "xu", "x", "d")
            if crossings[b] == 1:
                move(b, "xu", "d", ways(b)[1])
            then(b, "xu")

        def e7(b):
            got(b, "of", "od", "u")
            if crossings[b] == 2:
                got(b, "xf", "xd", "u")
            else:
                got(b, "xf", "xu", "d")
            then(b, "of")
            then(b, "xf")

        return e1, e2, e3, e4, e5, e6, e7

    def scatter(name, ref, land, crossings):
        def slot(b, k):
            return land.at[pl.ds(7 * FIRST[b] + k * RB[b], RB[b])]

        def push(b, chunk, k, device):
            start((name, b, k), ref.at[rows(b, side(b, chunk))], slot(b, k), device)

        def merge(b, chunk, slots, k, device):
            for each in slots:
                arrive((name, b, each), slot(b, each), UP)
            total = ref[rows(b, side(b, chunk)), :].astype(F32)
            for each in slots:
                total = total + slot(b, each)[...].astype(F32)
            at = slot(b, slots[0])
            at[...] = total.astype(BF16)
            start((name, b, k), at, slot(b, k), device)

        def last(b):
            return (3, 5, 6) if crossings[b] == 2 else (2, 5, 6)

        def f1(b):
            up, dn = ways(b)
            if crossings[b] == 2:
                push(b, "xf", 0, dn)
                push(b, "xu", 2, up)
                push(b, "of", 1, dn)
                push(b, "ou", 3, up)
            else:
                push(b, "xf", 0, up)
                push(b, "xd", 3, dn)
                push(b, "of", 1, dn)
                push(b, "ou", 2, up)

        def f2(b):
            if crossings[b] == 2:
                merge(b, "xd", (0,), 4, ACROSS)
            else:
                merge(b, "xu", (0,), 4, ways(b)[0])

        def f2b(b):
            if crossings[b] == 2:
                merge(b, "x", (2,), 5, ACROSS)
            else:
                merge(b, "od", (1,), 5, ways(b)[1])

        def f3(b):
            if crossings[b] == 2:
                merge(b, "od", (1, 4), 6, ways(b)[1])
            else:
                merge(b, "x", (3, 4), 6, ACROSS)

        def f4(b):
            for k in last(b):
                arrive((name, b, k), slot(b, k), UP)

        def result(b, first, size):
            at = pl.multiple_of(BASE[b] + j * RB[b] + first, 16)
            total = ref[pl.ds(at, size), :].astype(F32)
            for k in last(b):
                total = total + land[pl.ds(7 * FIRST[b] + k * RB[b] + first, size), :].astype(F32)
            return total

        return f1, f2, f2b, f3, f4, result

    ea = gather("a", tok, onward, CROSS["a"])
    eg = gather("g", go, lambda b, chunk: None, CROSS["g"])
    ra = scatter("r", gap, rs1, CROSS["r"])
    rg = scatter("s", peer, rs2, CROSS["s"])

    gain_row = gain[...].astype(F32)
    stale_row = stale_gain[...].astype(F32)

    def normalize(src, dst, at_dst, b, factor, keep):
        def body(at):
            values = src[pl.ds(pl.multiple_of(BASE[b] + at, 16), 16), :].astype(F32)
            scale = lax.rsqrt(jnp.mean(values * values, axis=-1, keepdims=True) + EPS)
            dst[pl.ds(pl.multiple_of(at_dst + at, 16), 16), :] = (values * scale * factor).astype(BF16)
            if keep:
                inv[pl.ds(pl.multiple_of(BASE[b] + at, 16), 16), :] = scale

        blocks(M[b], 16, body)

    def activate(b, ref, base, dst, at_dst):
        def body(at):
            r = pl.ds(pl.multiple_of(base + at, 16), 16)
            g, u = ref[r, left], ref[r, right]
            dst[pl.ds(pl.multiple_of(at_dst + at, 16), 16), :] = (g * jax.nn.sigmoid(g) * u).astype(BF16)

        blocks(M[b], 16, body)

    def p1(b):
        for chunk in pos:
            arrive(("n", b, chunk), tok_next.at[rows(b, chunk)], PREV)
        normalize(tok_next, xs, 0, b, stale_row, False)

    def p2(b):
        need("sg")
        need("su")
        own = pl.ds(0, M[b])
        gut[own, :] = dot_nn(xs[own, :], sgu[...])
        activate(b, gut, 0, hid_s, 0)

    def p4(b):
        need("sd")
        peer[batch(b), :] = dot_nn(hid_s[pl.ds(0, M[b]), :], sd[...]).astype(BF16)
        for half, device in ((0, NEXT), (1, NEXT_X)):
            r = pl.ds(BASE[b] + half * (M[b] // 2), M[b] // 2)
            start(("p", b, half), peer.at[r], gap.at[r], device)

    def o1(b):
        normalize(tok, x, BASE[b], b, gain_row, True)

    def o2(b):
        need("wg")
        need("wu")
        guv[batch(b), :] = dot_nn(x[batch(b), :], wgu[...])
        activate(b, guv, BASE[b], hid, BASE[b])

    def f0(b):
        need("wd")
        for half in range(2):
            arrive(("p", b, half), gap.at[pl.ds(BASE[b] + half * (M[b] // 2), M[b] // 2)], PREV)
        own = dot_nn(hid[batch(b), :], wd[...])
        gap[batch(b), :] = (own - gap[batch(b), :].astype(F32)).astype(BF16)
        ra[0](b)

    def f4(b):
        need("ups")
        ra[4](b)
        for first in range(0, RB[b], 16):
            total = ra[5](b, first, 16)
            mine = ups[pl.ds(FIRST[b] + first, 16), :].astype(F32) + AGREE * total
            go[pl.ds(pl.multiple_of(BASE[b] + j * RB[b] + first, 16), 16), :] = mine.astype(BF16)
        eg[0](b)

    def b1(b):
        gut[pl.ds(0, M[b]), left] = dot_nt(go[batch(b), :], wd[...])

        def body(at):
            r = pl.ds(pl.multiple_of(BASE[b] + at, 16), 16)
            g, u = guv[r, left], guv[r, right]
            s = jax.nn.sigmoid(g)
            gh = gut[pl.ds(at, 16), left]
            gp[r, left] = (gh * u * s * (1.0 + g * (1.0 - s))).astype(BF16)
            gp[r, right] = (gh * (g * s)).astype(BF16)

        blocks(M[b], 16, body)

    waited = set()

    def b2(b):
        for key, copy in sent:
            if key[:2] == ("p", b):
                copy.wait_send()
                waited.add(key)
        peer[batch(b), :] = dot_nt(gp[batch(b), :], wgu[...]).astype(BF16)
        rg[0](b)

    def b4(b):
        def body(at):
            r = pl.ds(pl.multiple_of(BASE[b] + at, 16), 16)
            part = peer[r, :].astype(F32) * (tok[r, :].astype(F32) * inv[r, :])
            acc[...] += part[:8] + part[8:]

        blocks(M[b], 16, body)

    def k1(b):
        acc_out[...] = jnp.sum(acc[...], axis=0, keepdims=True)
        for step in range(1, N):
            start(("k", step), acc_out, acc_in.at[step], (member, (j + step) % N))

    def k2(b):
        total = acc_out[...]
        for step in range(1, N):
            arrive(("k", step), acc_in.at[step], (member, (j + step) % N))
            total = total + acc_in[step]
        gain_buf[...] = total
        fetch("ok", gain_buf, out_gain)

    def f4g(b):
        rg[4](b)
        for first in range(0, RB[b], 16):
            grad_in = rg[5](b, first, 16)
            r = pl.ds(pl.multiple_of(BASE[b] + j * RB[b] + first, 16), 16)
            scale = inv[r, :]
            normed = tok[r, :].astype(F32) * scale
            grad_normed = grad_in * gain_row
            mean = jnp.mean(grad_normed * normed, axis=-1, keepdims=True)
            if b < NB - 1:
                part = grad_in * normed
                acc[...] += part[:8] + part[8:]
            outt[pl.ds(FIRST[b] + first, 16), :] = (
                go[r, :].astype(F32) + scale * (grad_normed - normed * mean)
            ).astype(BF16)
        r = pl.ds(FIRST[b], RB[b])
        fetch(("ot", b), outt.at[r], out_tokens.at[0, r])

    def weight_down(i):
        r = pl.ds(i * 256, 256)
        sd[r, :] = dot_tn(hid[:, i * 256 : (i + 1) * 256], go[...]).astype(BF16)
        fetch(("d", i), sd.at[r], out_down.at[0, r])

    def weight_up(i):
        r = pl.ds(i * 256, 256)
        sgu[r, :] = dot_tn(x[:, i * 256 : (i + 1) * 256], gp[...]).astype(BF16)
        fetch(("g", i), sgu.at[r, left], out_gate.at[0, r])
        fetch(("u", i), sgu.at[r, right], out_up.at[0, r])

    def n1(b):
        onward(b, "o")

    tasks = {
        "N": n1,
        "P1": p1, "P2": p2, "P4": p4, "O1": o1, "O2": o2, "F0": f0, "F4": f4,
        "F2": ra[1], "F2b": ra[2], "F3": ra[3], "S2": rg[1], "S2b": rg[2], "S3": rg[3], "S4": f4g,
        "B1": b1, "B2": b2, "B4": b4, "K1": k1, "K2": k2, "WD": weight_down, "WU": weight_up,
    }
    for i in range(7):
        tasks["E%d" % (i + 1)] = ea[i]
        tasks["G%d" % (i + 1)] = eg[i]
    for name, index in ORDER:
        tasks[name](index)

    for key, copy in sent:
        if key not in waited:
            copy.wait_send()
    for key in locals_:
        need(key)


def hand_over(*refs):
    sources, results, holds, sems = refs[:5], refs[5:10], refs[10:15], refs[15]
    steps = []
    for i, (src, hold, dst) in enumerate(zip(sources, holds, results)):
        whole = src.shape[1]
        parts = 4 if 0 < i < 4 else 1
        for part in range(parts):
            r = pl.ds(part * (whole // parts), whole // parts)
            steps.append((
                pltpu.make_async_copy(src.at[:, r], hold.at[:, r], sems.at[0, i, part]),
                pltpu.make_async_copy(hold.at[:, r], dst.at[:, r], sems.at[1, i, part]),
            ))
    for first, _ in steps:
        first.start()
    for first, second in steps:
        first.wait()
        second.start()
    for _, second in steps:
        second.wait()


def shards(
    tokens, upstream, gate_weight, up_weight, down_weight, norm_gain,
    stale_gate, stale_up, stale_down, stale_gain,
):
    hbm = pl.BlockSpec(memory_space=pl.ANY)
    vmem = pl.BlockSpec(memory_space=pltpu.VMEM)
    total = N * ROWS
    wide = pltpu.VMEM((total, D), BF16)
    half = pltpu.VMEM((total, FB), BF16)
    square = pltpu.VMEM((D, D), BF16)
    flat = pltpu.VMEM((FB, D), BF16)
    land = pltpu.VMEM((7 * ROWS, D), BF16)
    results = (
        jax.ShapeDtypeStruct((1, ROWS, D), BF16),
        jax.ShapeDtypeStruct((1, D, FB), BF16),
        jax.ShapeDtypeStruct((1, D, FB), BF16),
        jax.ShapeDtypeStruct((1, FB, D), BF16),
        jax.ShapeDtypeStruct((1, D), F32),
    )
    parts = pl.pallas_call(
        kernel,
        out_shape=results,
        in_specs=[hbm, hbm, hbm, hbm, hbm, vmem, hbm, hbm, hbm, vmem],
        out_specs=(hbm,) * 5,
        scratch_shapes=[
            square, flat, square, flat,
            pltpu.VMEM((ROWS, D), BF16),
            wide, wide, wide,
            pltpu.VMEM((max(M), D), BF16),
            pltpu.VMEM((total, 1), F32),
            pltpu.VMEM((total, D), F32), pltpu.VMEM((max(M), D), F32), half,
            pltpu.VMEM((max(M), FB), BF16),
            wide, wide, land, land, wide, wide,
            pltpu.VMEM((ROWS, D), BF16),
            pltpu.VMEM((8, D), F32),
            pltpu.VMEM((1, D), F32),
            pltpu.VMEM((N, 1, D), F32),
            pltpu.VMEM((1, D), F32),
            pltpu.SemaphoreType.DMA((NB * 38 + 8,)),
            pltpu.SemaphoreType.DMA((NB * 38 + 8,)),
            pltpu.SemaphoreType.DMA((2 * NB + 7 + 16,)),
        ],
        compiler_params=pltpu.CompilerParams(
            collective_id=0, has_side_effects=True, vmem_limit_bytes=62 * 2**20
        ),
        name="layer",
    )(
        tokens, upstream, gate_weight, up_weight, down_weight, norm_gain,
        stale_gate, stale_up, stale_down, stale_gain,
    )
    return pl.pallas_call(
        hand_over,
        out_shape=results,
        in_specs=[hbm] * 5,
        out_specs=(hbm,) * 5,
        scratch_shapes=[pltpu.VMEM(r.shape, r.dtype) for r in results]
        + [pltpu.SemaphoreType.DMA((2, 5, 4))],
        compiler_params=pltpu.CompilerParams(vmem_limit_bytes=62 * 2**20),
        name="hand_over",
    )(*parts)


def solution(mesh):
    in_specs = (
        P("member", "fsdp", None),
        P("member", "fsdp", None),
        P("member", None, "fsdp"),
        P("member", None, "fsdp"),
        P("member", "fsdp", None),
        P("member", None),
        P("member", None, "fsdp"),
        P("member", None, "fsdp"),
        P("member", "fsdp", None),
        P("member", None),
    )
    out_specs = (
        P("member", "fsdp", None),
        P("member", None, "fsdp"),
        P("member", None, "fsdp"),
        P("member", "fsdp", None),
        P("member", None),
    )
    return jax.shard_map(shards, mesh=mesh, in_specs=in_specs, out_specs=out_specs, check_vma=False)
```

```python
import functools
import jax
import jax.numpy as jnp
from jax import lax
from jax.experimental import pallas as pl
from jax.experimental.pallas import tpu as pltpu
from jax.sharding import PartitionSpec as P

EPS = 1e-05
AGREE = 1.0
MESH = pl.DeviceIdType.MESH
F32 = jnp.float32
BF16 = jnp.bfloat16
D = 1536
FB = 768
N = 8
ROWS = 128
RB = (16, 16, 32, 32, 32)
NB = len(RB)
FIRST = tuple(sum(RB[:b]) for b in range(NB))
CROSS = {"a": (1,) * 5, "r": (1, 1, 1, 1, 1), "g": (1, 1, 2, 2, 2), "s": (2,) * 5}
M = tuple(N * size for size in RB)
BASE = tuple(N * first for first in FIRST)

ORDER = (
    ("E1", 0), ("N", 2), ("E1", 1), ("N", 1), ("E1", 2), ("E3", 0), ("E2", 0), ("E5", 1), ("E3", 1),
    ("E2", 2), ("E4", 0), ("E5", 0), ("E6", 0), ("E3", 2), ("E7", 0), ("E5", 2), ("E2", 1), ("O1", 0),
    ("E6", 1), ("O2", 0), ("E6", 2), ("P1", 0), ("E1", 3), ("E1", 4), ("E4", 1), ("P2", 0), ("E7", 1),
    ("P4", 0), ("O1", 1), ("E4", 2), ("E7", 2), ("P1", 1), ("E3", 3), ("P2", 1), ("P4", 1), ("E2", 3),
    ("P1", 2), ("E5", 3), ("E6", 3), ("N", 4), ("N", 3), ("P2", 2), ("F0", 0), ("P4", 2), ("O2", 1),
    ("E3", 4), ("E4", 3), ("E7", 3), ("F2", 0), ("F0", 1), ("O1", 2), ("O2", 2), ("F2", 1), ("P1", 3),
    ("F3", 0), ("E5", 4), ("P2", 3), ("F2b", 1), ("E6", 4), ("F3", 1), ("P4", 3), ("E2", 4), ("E4", 4),
    ("F0", 2), ("O1", 3), ("F2b", 0), ("E7", 4), ("O2", 3), ("F2", 2), ("P1", 4), ("F4", 0), ("F4", 1),
    ("F2b", 2), ("P2", 4), ("P4", 4), ("G2", 0), ("F3", 2), ("F0", 3), ("G3", 0), ("G3", 1), ("G2", 1),
    ("F2b", 3), ("G5", 0), ("O1", 4), ("F2", 3), ("G6", 0), ("G5", 1), ("G4", 1), ("G6", 1), ("F4", 2),
    ("O2", 4), ("F0", 4), ("G4", 0), ("G7", 0), ("B1", 0), ("F3", 3), ("F2", 4), ("B2", 0), ("G2", 2),
    ("F3", 4), ("G7", 1), ("F2b", 4), ("G3", 2), ("F4", 3), ("G4", 2), ("B1", 1), ("F4", 4), ("G5", 2),
    ("G3", 3), ("G2", 3), ("B2", 1), ("G6", 2), ("S2b", 0), ("G7", 2), ("B1", 2), ("G2", 4), ("G5", 3),
    ("S2", 0), ("G4", 3), ("G6", 3), ("G5", 4), ("B2", 2), ("S2", 1), ("G7", 3), ("B1", 3), ("S2b", 2),
    ("G3", 4), ("S2", 2), ("G4", 4), ("S3", 0), ("B2", 3), ("S3", 1), ("S2b", 1), ("G6", 4), ("G7", 4),
    ("B1", 4), ("B2", 4), ("S2", 3), ("WU", 4), ("WU", 2), ("S4", 0), ("S2b", 3), ("WD", 1), ("WD", 0),
    ("S3", 3), ("S4", 1), ("S3", 2), ("S2", 4), ("WU", 0), ("WD", 2), ("S2b", 4), ("B4", 4), ("S4", 3),
    ("S4", 2), ("K1", 0), ("S3", 4), ("WU", 1), ("WU", 5), ("WU", 3), ("S4", 4), ("K2", 0),
)


def dot_nn(a, b):
    return jnp.dot(a, b, preferred_element_type=F32)


def dot_nt(a, b):
    return lax.dot_general(a, b, (((1,), (1,)), ((), ())), preferred_element_type=F32)


def dot_tn(a, b):
    return lax.dot_general(a, b, (((0,), (0,)), ((), ())), preferred_element_type=F32)


def blocks(total, size, body):
    @pl.loop(0, total // size)
    def _(i):
        body(pl.multiple_of(i * size, size))


def kernel(
    tokens, upstream, gate_w, up_w, down_w, gain, stale_gate, stale_up, stale_down, stale_gain,
    out_tokens, out_gate, out_up, out_down, out_gain,
    wgu, wd, sgu, sd, ups, tok, tok_next, x, xs, inv, guv, gut, hid, hid_s,
    gap, peer, rs1, rs2, go, gp, outt, acc, acc_out, acc_in, gain_buf,
    send, recv, local,
):
    member = lax.axis_index("member")
    j = lax.axis_index("fsdp")
    y, z = j // 4, j % 4
    members = lax.axis_size("member")
    z_up, z_dn, z_far = (z + 1) % 4, (z + 3) % 4, (z + 2) % 4
    other = 1 - y
    UP, DN, ACROSS = (member, y * 4 + z_up), (member, y * 4 + z_dn), (member, other * 4 + z)
    NEXT = ((member + 1) % members, j)
    PREV = ((member + members - 1) % members, j)
    edge_prev, edge_next = ((member + 7) % 8) // 7, (member % 8) // 7
    PREV_X = (PREV[0], ((y + edge_prev) % 2) * 4 + z)
    NEXT_X = (NEXT[0], ((y + edge_next) % 2) * 4 + z)

    pos = {
        "o": j,
        "ou": y * 4 + z_up,
        "od": y * 4 + z_dn,
        "of": y * 4 + z_far,
        "x": other * 4 + z,
        "xu": other * 4 + z_up,
        "xd": other * 4 + z_dn,
        "xf": other * 4 + z_far,
    }

    def rows(b, chunk):
        return pl.ds(pl.multiple_of(BASE[b] + pos[chunk] * RB[b], 16), RB[b])

    def batch(b):
        return pl.ds(BASE[b], M[b])

    numbers = {}

    def number(key):
        return numbers.setdefault(key, len(numbers))

    def remote(key, src, dst, device):
        i = number(key)
        return pltpu.make_async_remote_copy(
            src_ref=src,
            dst_ref=dst,
            send_sem=send.at[i],
            recv_sem=recv.at[i],
            device_id=device,
            device_id_type=MESH,
        )

    sent = []

    def start(key, src, dst, device):
        copy = remote(key, src, dst, device)
        copy.start()
        sent.append((key, copy))

    def arrive(key, dst, device):
        remote(key, dst, dst, device).wait_recv()

    locals_ = {}

    def fetch(key, src, dst):
        copy = pltpu.make_async_copy(src, dst, local.at[len(locals_)])
        locals_[key] = copy
        copy.start()

    done = set()

    def need(key):
        if key not in done:
            done.add(key)
            locals_[key].wait()

    barrier = pltpu.get_barrier_semaphore()
    for step in range(1, N):
        pl.semaphore_signal(barrier, inc=1, device_id=(member, (j + step) % N), device_id_type=MESH)
    for to in (NEXT[0], PREV[0]):
        for at in (y, other):
            pl.semaphore_signal(barrier, inc=1, device_id=(to, at * 4 + z), device_id_type=MESH)
    for b in range(NB):
        fetch(("t", b), tokens.at[0, pl.ds(FIRST[b], RB[b])], tok.at[rows(b, "o")])
    left, right = pl.ds(0, FB), pl.ds(FB, FB)
    fetch("sg", stale_gate.at[0], sgu.at[:, left])
    fetch("su", stale_up.at[0], sgu.at[:, right])
    fetch("sd", stale_down.at[0], sd)
    fetch("wg", gate_w.at[0], wgu.at[:, left])
    fetch("wu", up_w.at[0], wgu.at[:, right])
    fetch("wd", down_w.at[0], wd)
    fetch("ups", upstream.at[0], ups)
    acc[...] = jnp.zeros_like(acc)
    pl.semaphore_wait(barrier, N + 3)

    mirror = {"ou": "od", "od": "ou", "xu": "xd", "xd": "xu"}

    def side(b, chunk):
        return mirror.get(chunk, chunk) if b % 2 else chunk

    def ways(b):
        return (DN, UP) if b % 2 else (UP, DN)

    def onward(b, chunk):
        chunk = side(b, chunk)
        if chunk[0] == "o":
            start(("n", b, chunk), tok.at[rows(b, chunk)], tok_next.at[rows(b, chunk)], PREV)
        else:
            at = ((other + edge_prev) % 2) * 4 + pos[chunk] % 4
            r = pl.ds(pl.multiple_of(BASE[b] + at * RB[b], 16), RB[b])
            start(("n", b, chunk), tok.at[r], tok_next.at[r], PREV_X)

    def gather(name, ref, then, crossings):
        def move(b, chunk, way, device):
            r = rows(b, side(b, chunk))
            start((name, b, chunk, way), ref.at[r], ref.at[r], device)

        def got(b, chunk, sent_as, way):
            arrive((name, b, sent_as, way), ref.at[rows(b, side(b, chunk))], UP)

        def e1(b):
            up, dn = ways(b)
            if name == "g":
                move(b, "o", "a", ACROSS)
            elif b == 0:
                for each in range(NB):
                    need(("t", each))
                    move(each, "o", "a", ACROSS)
                    if each == 0:
                        move(b, "o", "u", up)
                        move(b, "o", "d", dn)
                then(b, "o")
                return
            move(b, "o", "u", up)
            move(b, "o", "d", dn)

        def e2(b):
            got(b, "od", "o", "u")
            if crossings[b] == 2:
                move(b, "od", "a", ACROSS)
            move(b, "od", "u", ways(b)[0])
            then(b, "od")

        def e3(b):
            got(b, "x", "o", "a")
            move(b, "x", "d", ways(b)[1])
            if crossings[b] == 1:
                move(b, "x", "u", ways(b)[0])
            then(b, "x")

        def e4(b):
            if crossings[b] == 2:
                got(b, "xd", "od", "a")
                move(b, "xd", "u", ways(b)[0])
            else:
                got(b, "xd", "x", "u")
            then(b, "xd")

        def e5(b):
            got(b, "ou", "o", "d")
            then(b, "ou")

        def e6(b):
            got(b, "xu", "x", "d")
            if crossings[b] == 1:
                move(b, "xu", "d", ways(b)[1])
            then(b, "xu")

        def e7(b):
            got(b, "of", "od", "u")
            if crossings[b] == 2:
                got(b, "xf", "xd", "u")
            else:
                got(b, "xf", "xu", "d")
            then(b, "of")
            then(b, "xf")

        return e1, e2, e3, e4, e5, e6, e7

    def scatter(name, ref, land, crossings):
        def slot(b, k):
            return land.at[pl.ds(7 * FIRST[b] + k * RB[b], RB[b])]

        def push(b, chunk, k, device):
            start((name, b, k), ref.at[rows(b, side(b, chunk))], slot(b, k), device)

        def merge(b, chunk, slots, k, device):
            for each in slots:
                arrive((name, b, each), slot(b, each), UP)
            total = ref[rows(b, side(b, chunk)), :].astype(F32)
            for each in slots:
                total = total + slot(b, each)[...].astype(F32)
            at = slot(b, slots[0])
            at[...] = total.astype(BF16)
            start((name, b, k), at, slot(b, k), device)

        def last(b):
            return (3, 5, 6) if crossings[b] == 2 else (2, 5, 6)

        def f1(b):
            up, dn = ways(b)
            if crossings[b] == 2:
                push(b, "xf", 0, dn)
                push(b, "xu", 2, up)
                push(b, "of", 1, dn)
                push(b, "ou", 3, up)
            else:
                push(b, "xf", 0, up)
                push(b, "xd", 3, dn)
                push(b, "of", 1, dn)
                push(b, "ou", 2, up)

        def f2(b):
            if crossings[b] == 2:
                merge(b, "xd", (0,), 4, ACROSS)
            else:
                merge(b, "xu", (0,), 4, ways(b)[0])

        def f2b(b):
            if crossings[b] == 2:
                merge(b, "x", (2,), 5, ACROSS)
            else:
                merge(b, "od", (1,), 5, ways(b)[1])

        def f3(b):
            if crossings[b] == 2:
                merge(b, "od", (1, 4), 6, ways(b)[1])
            else:
                merge(b, "x", (3, 4), 6, ACROSS)

        def f4(b):
            for k in last(b):
                arrive((name, b, k), slot(b, k), UP)

        def result(b, first, size):
            at = pl.multiple_of(BASE[b] + j * RB[b] + first, 16)
            total = ref[pl.ds(at, size), :].astype(F32)
            for k in last(b):
                total = total + land[pl.ds(7 * FIRST[b] + k * RB[b] + first, size), :].astype(F32)
            return total

        return f1, f2, f2b, f3, f4, result

    ea = gather("a", tok, onward, CROSS["a"])
    eg = gather("g", go, lambda b, chunk: None, CROSS["g"])
    ra = scatter("r", gap, rs1, CROSS["r"])
    rg = scatter("s", peer, rs2, CROSS["s"])

    gain_row = gain[...].astype(F32)
    stale_row = stale_gain[...].astype(F32)

    def normalize(src, dst, at_dst, b, factor, keep):
        def body(at):
            values = src[pl.ds(pl.multiple_of(BASE[b] + at, 16), 16), :].astype(F32)
            scale = lax.rsqrt(jnp.mean(values * values, axis=-1, keepdims=True) + EPS)
            dst[pl.ds(pl.multiple_of(at_dst + at, 16), 16), :] = (values * scale * factor).astype(BF16)
            if keep:
                inv[pl.ds(pl.multiple_of(BASE[b] + at, 16), 16), :] = scale

        blocks(M[b], 16, body)

    def activate(b, ref, base, dst, at_dst):
        def body(at):
            r = pl.ds(pl.multiple_of(base + at, 16), 16)
            g, u = ref[r, left], ref[r, right]
            dst[pl.ds(pl.multiple_of(at_dst + at, 16), 16), :] = (g * jax.nn.sigmoid(g) * u).astype(BF16)

        blocks(M[b], 16, body)

    def p1(b):
        for chunk in pos:
            arrive(("n", b, chunk), tok_next.at[rows(b, chunk)], PREV)
        normalize(tok_next, xs, 0, b, stale_row, False)

    def p2(b):
        need("sg")
        need("su")
        own = pl.ds(0, M[b])
        gut[own, :] = dot_nn(xs[own, :], sgu[...])
        activate(b, gut, 0, hid_s, 0)

    def p4(b):
        need("sd")
        peer[batch(b), :] = dot_nn(hid_s[pl.ds(0, M[b]), :], sd[...]).astype(BF16)
        for half, device in ((0, NEXT), (1, NEXT_X)):
            r = pl.ds(BASE[b] + half * (M[b] // 2), M[b] // 2)
            start(("p", b, half), peer.at[r], gap.at[r], device)

    def o1(b):
        normalize(tok, x, BASE[b], b, gain_row, True)

    def o2(b):
        need("wg")
        need("wu")
        guv[batch(b), :] = dot_nn(x[batch(b), :], wgu[...])
        activate(b, guv, BASE[b], hid, BASE[b])

    def f0(b):
        need("wd")
        for half in range(2):
            arrive(("p", b, half), gap.at[pl.ds(BASE[b] + half * (M[b] // 2), M[b] // 2)], PREV)
        own = dot_nn(hid[batch(b), :], wd[...])
        gap[batch(b), :] = (own - gap[batch(b), :].astype(F32)).astype(BF16)
        ra[0](b)

    def f4(b):
        need("ups")
        ra[4](b)
        for first in range(0, RB[b], 16):
            total = ra[5](b, first, 16)
            mine = ups[pl.ds(FIRST[b] + first, 16), :].astype(F32) + AGREE * total
            go[pl.ds(pl.multiple_of(BASE[b] + j * RB[b] + first, 16), 16), :] = mine.astype(BF16)
        eg[0](b)

    def b1(b):
        gut[pl.ds(0, M[b]), left] = dot_nt(go[batch(b), :], wd[...])

        def body(at):
            r = pl.ds(pl.multiple_of(BASE[b] + at, 16), 16)
            g, u = guv[r, left], guv[r, right]
            s = jax.nn.sigmoid(g)
            gh = gut[pl.ds(at, 16), left]
            gp[r, left] = (gh * u * s * (1.0 + g * (1.0 - s))).astype(BF16)
            gp[r, right] = (gh * (g * s)).astype(BF16)

        blocks(M[b], 16, body)

    waited = set()

    def b2(b):
        for key, copy in sent:
            if key[:2] == ("p", b):
                copy.wait_send()
                waited.add(key)
        peer[batch(b), :] = dot_nt(gp[batch(b), :], wgu[...]).astype(BF16)
        rg[0](b)

    def b4(b):
        def body(at):
            r = pl.ds(pl.multiple_of(BASE[b] + at, 16), 16)
            part = peer[r, :].astype(F32) * (tok[r, :].astype(F32) * inv[r, :])
            acc[...] += part[:8] + part[8:]

        blocks(M[b], 16, body)

    def k1(b):
        acc_out[...] = jnp.sum(acc[...], axis=0, keepdims=True)
        for step in range(1, N):
            start(("k", step), acc_out, acc_in.at[step], (member, (j + step) % N))

    def k2(b):
        total = acc_out[...]
        for step in range(1, N):
            arrive(("k", step), acc_in.at[step], (member, (j + step) % N))
            total = total + acc_in[step]
        gain_buf[...] = total
        fetch("ok", gain_buf, out_gain)

    def f4g(b):
        rg[4](b)
        for first in range(0, RB[b], 16):
            grad_in = rg[5](b, first, 16)
            r = pl.ds(pl.multiple_of(BASE[b] + j * RB[b] + first, 16), 16)
            scale = inv[r, :]
            normed = tok[r, :].astype(F32) * scale
            grad_normed = grad_in * gain_row
            mean = jnp.mean(grad_normed * normed, axis=-1, keepdims=True)
            if b < NB - 1:
                part = grad_in * normed
                acc[...] += part[:8] + part[8:]
            outt[pl.ds(FIRST[b] + first, 16), :] = (
                go[r, :].astype(F32) + scale * (grad_normed - normed * mean)
            ).astype(BF16)
        r = pl.ds(FIRST[b], RB[b])
        fetch(("ot", b), outt.at[r], out_tokens.at[0, r])

    def weight_down(i):
        r = pl.ds(i * 256, 256)
        sd[r, :] = dot_tn(hid[:, i * 256 : (i + 1) * 256], go[...]).astype(BF16)
        fetch(("d", i), sd.at[r], out_down.at[0, r])

    def weight_up(i):
        r = pl.ds(i * 256, 256)
        sgu[r, :] = dot_tn(x[:, i * 256 : (i + 1) * 256], gp[...]).astype(BF16)
        fetch(("g", i), sgu.at[r, left], out_gate.at[0, r])
        fetch(("u", i), sgu.at[r, right], out_up.at[0, r])

    def n1(b):
        onward(b, "o")

    tasks = {
        "N": n1,
        "P1": p1, "P2": p2, "P4": p4, "O1": o1, "O2": o2, "F0": f0, "F4": f4,
        "F2": ra[1], "F2b": ra[2], "F3": ra[3], "S2": rg[1], "S2b": rg[2], "S3": rg[3], "S4": f4g,
        "B1": b1, "B2": b2, "B4": b4, "K1": k1, "K2": k2, "WD": weight_down, "WU": weight_up,
    }
    for i in range(7):
        tasks["E%d" % (i + 1)] = ea[i]
        tasks["G%d" % (i + 1)] = eg[i]
    for name, index in ORDER:
        tasks[name](index)

    for key, copy in sent:
        if key not in waited:
            copy.wait_send()
    for key in locals_:
        need(key)


def hand_over(*refs):
    sources, results, holds, sems = refs[:5], refs[5:10], refs[10:15], refs[15]
    steps = []
    for i, (src, hold, dst) in enumerate(zip(sources, holds, results)):
        whole = src.shape[1]
        parts = 4 if 0 < i < 4 else 1
        for part in range(parts):
            r = pl.ds(part * (whole // parts), whole // parts)
            steps.append((
                pltpu.make_async_copy(src.at[:, r], hold.at[:, r], sems.at[0, i, part]),
                pltpu.make_async_copy(hold.at[:, r], dst.at[:, r], sems.at[1, i, part]),
            ))
    ahead = 5
    for first, _ in steps[:ahead]:
        first.start()
    for i, (first, second) in enumerate(steps):
        first.wait()
        second.start()
        if i + ahead < len(steps):
            steps[i + ahead][0].start()
    for _, second in steps:
        second.wait()


def shards(
    tokens, upstream, gate_weight, up_weight, down_weight, norm_gain,
    stale_gate, stale_up, stale_down, stale_gain,
):
    hbm = pl.BlockSpec(memory_space=pl.ANY)
    vmem = pl.BlockSpec(memory_space=pltpu.VMEM)
    total = N * ROWS
    wide = pltpu.VMEM((total, D), BF16)
    half = pltpu.VMEM((total, FB), BF16)
    square = pltpu.VMEM((D, D), BF16)
    flat = pltpu.VMEM((FB, D), BF16)
    land = pltpu.VMEM((7 * ROWS, D), BF16)
    results = (
        jax.ShapeDtypeStruct((1, ROWS, D), BF16),
        jax.ShapeDtypeStruct((1, D, FB), BF16),
        jax.ShapeDtypeStruct((1, D, FB), BF16),
        jax.ShapeDtypeStruct((1, FB, D), BF16),
        jax.ShapeDtypeStruct((1, D), F32),
    )
    parts = pl.pallas_call(
        kernel,
        out_shape=results,
        in_specs=[hbm, hbm, hbm, hbm, hbm, vmem, hbm, hbm, hbm, vmem],
        out_specs=(hbm,) * 5,
        scratch_shapes=[
            square, flat, square, flat,
            pltpu.VMEM((ROWS, D), BF16),
            wide, wide, wide,
            pltpu.VMEM((max(M), D), BF16),
            pltpu.VMEM((total, 1), F32),
            pltpu.VMEM((total, D), F32), pltpu.VMEM((max(M), D), F32), half,
            pltpu.VMEM((max(M), FB), BF16),
            wide, wide, land, land, wide, wide,
            pltpu.VMEM((ROWS, D), BF16),
            pltpu.VMEM((8, D), F32),
            pltpu.VMEM((1, D), F32),
            pltpu.VMEM((N, 1, D), F32),
            pltpu.VMEM((1, D), F32),
            pltpu.SemaphoreType.DMA((NB * 38 + 8,)),
            pltpu.SemaphoreType.DMA((NB * 38 + 8,)),
            pltpu.SemaphoreType.DMA((2 * NB + 7 + 16,)),
        ],
        compiler_params=pltpu.CompilerParams(
            collective_id=0, has_side_effects=True, vmem_limit_bytes=62 * 2**20
        ),
        name="layer",
    )(
        tokens, upstream, gate_weight, up_weight, down_weight, norm_gain,
        stale_gate, stale_up, stale_down, stale_gain,
    )
    return pl.pallas_call(
        hand_over,
        out_shape=results,
        in_specs=[hbm] * 5,
        out_specs=(hbm,) * 5,
        scratch_shapes=[pltpu.VMEM(r.shape, r.dtype) for r in results]
        + [pltpu.SemaphoreType.DMA((2, 5, 4))],
        compiler_params=pltpu.CompilerParams(vmem_limit_bytes=62 * 2**20),
        name="hand_over",
    )(*parts)


def solution(mesh):
    in_specs = (
        P("member", "fsdp", None),
        P("member", "fsdp", None),
        P("member", None, "fsdp"),
        P("member", None, "fsdp"),
        P("member", "fsdp", None),
        P("member", None),
        P("member", None, "fsdp"),
        P("member", None, "fsdp"),
        P("member", "fsdp", None),
        P("member", None),
    )
    out_specs = (
        P("member", "fsdp", None),
        P("member", None, "fsdp"),
        P("member", None, "fsdp"),
        P("member", "fsdp", None),
        P("member", None),
    )
    return jax.shard_map(shards, mesh=mesh, in_specs=in_specs, out_specs=out_specs, check_vma=False)
```

```python
import functools
import jax
import jax.numpy as jnp
from jax import lax
from jax.experimental import pallas as pl
from jax.experimental.pallas import tpu as pltpu
from jax.sharding import PartitionSpec as P

EPS = 1e-05
AGREE = 1.0
MESH = pl.DeviceIdType.MESH
F32 = jnp.float32
BF16 = jnp.bfloat16
D = 1536
FB = 768
N = 8
ROWS = 128
RB = (16, 16, 32, 32, 32)
NB = len(RB)
FIRST = tuple(sum(RB[:b]) for b in range(NB))
CROSS = {"a": (1,) * 5, "r": (1, 1, 1, 1, 2), "g": (1, 1, 2, 2, 2), "s": (2,) * 5}
M = tuple(N * size for size in RB)
BASE = tuple(N * first for first in FIRST)

ORDER = (
    ("E1", 0), ("E1", 1), ("E1", 2), ("N", 1), ("N", 2), ("E2", 0), ("E5", 0), ("E5", 1), ("E3", 0),
    ("E3", 1), ("E5", 2), ("E6", 0), ("E3", 2), ("E4", 0), ("E7", 0), ("E2", 1), ("E6", 1), ("E2", 2),
    ("O1", 0), ("E1", 3), ("E4", 1), ("O2", 0), ("E6", 2), ("P1", 0), ("P2", 0), ("E7", 1), ("E4", 2),
    ("P4", 0), ("E7", 2), ("E3", 3), ("E1", 4), ("E5", 3), ("O1", 1), ("P1", 1), ("P2", 1), ("P4", 1),
    ("E3", 4), ("E2", 3), ("N", 3), ("P1", 2), ("E6", 3), ("P2", 2), ("E4", 3), ("P4", 2), ("E2", 4),
    ("F0", 0), ("O2", 1), ("F0", 1), ("E7", 3), ("O1", 2), ("E5", 4), ("E6", 4), ("O1", 3), ("F2", 0),
    ("F2", 1), ("P1", 3), ("P2", 3), ("F3", 0), ("E7", 4), ("F3", 1), ("E4", 4), ("F2b", 1), ("P4", 3),
    ("F2b", 0), ("N", 4), ("O2", 2), ("F0", 2), ("O2", 3), ("P1", 4), ("F2", 2), ("F4", 0), ("F2b", 2),
    ("P2", 4), ("F4", 1), ("F3", 2), ("F0", 3), ("P4", 4), ("G2", 0), ("G3", 1), ("G2", 1), ("G3", 0),
    ("F2b", 3), ("F4", 2), ("O1", 4), ("G5", 1), ("G5", 0), ("G4", 0), ("G6", 0), ("F2", 3), ("G6", 1),
    ("O2", 4), ("G5", 2), ("F0", 4), ("G2", 2), ("G7", 1), ("G4", 1), ("F3", 3), ("G7", 0), ("B1", 0),
    ("G3", 2), ("B2", 0), ("F2", 4), ("B1", 1), ("G4", 2), ("F2b", 4), ("F4", 3), ("F3", 4), ("B2", 1),
    ("G2", 3), ("F4", 4), ("G5", 3), ("G3", 3), ("G6", 2), ("G7", 2), ("G4", 3), ("S2", 1), ("B1", 2),
    ("G2", 4), ("B2", 2), ("G3", 4), ("G6", 3), ("S2", 0), ("G4", 4), ("S2b", 0), ("S2", 2), ("S3", 1),
    ("G5", 4), ("S2b", 1), ("S2b", 2), ("G7", 3), ("B1", 3), ("S3", 0), ("B2", 3), ("G7", 4), ("G6", 4),
    ("B1", 4), ("S4", 0), ("B2", 4), ("S2", 3), ("S2b", 3), ("B4", 4), ("WD", 2), ("S3", 2), ("WU", 5),
    ("WD", 0), ("S3", 3), ("S2", 4), ("WD", 1), ("WU", 4), ("WU", 2), ("S2b", 4), ("S4", 1), ("S4", 2),
    ("S4", 3), ("K1", 0), ("S3", 4), ("WU", 0), ("WU", 1), ("WU", 3), ("S4", 4), ("K2", 0),
)


def dot_nn(a, b):
    return jnp.dot(a, b, preferred_element_type=F32)


def dot_nt(a, b):
    return lax.dot_general(a, b, (((1,), (1,)), ((), ())), preferred_element_type=F32)


def dot_tn(a, b):
    return lax.dot_general(a, b, (((0,), (0,)), ((), ())), preferred_element_type=F32)


def blocks(total, size, body):
    @pl.loop(0, total // size)
    def _(i):
        body(pl.multiple_of(i * size, size))


def kernel(
    tokens, upstream, gate_w, up_w, down_w, gain, stale_gate, stale_up, stale_down, stale_gain,
    out_tokens, out_gate, out_up, out_down, out_gain,
    wgu, wd, sgu, sd, ups, tok, tok_next, x, xs, inv, guv, gut, hid, hid_s,
    gap, peer, rs1, rs2, go, gp, outt, acc, acc_out, acc_in, gain_buf,
    send, recv, local,
):
    member = lax.axis_index("member")
    j = lax.axis_index("fsdp")
    y, z = j // 4, j % 4
    members = lax.axis_size("member")
    z_up, z_dn, z_far = (z + 1) % 4, (z + 3) % 4, (z + 2) % 4
    other = 1 - y
    UP, DN, ACROSS = (member, y * 4 + z_up), (member, y * 4 + z_dn), (member, other * 4 + z)
    NEXT = ((member + 1) % members, j)
    PREV = ((member + members - 1) % members, j)
    edge_prev, edge_next = ((member + 7) % 8) // 7, (member % 8) // 7
    PREV_X = (PREV[0], ((y + edge_prev) % 2) * 4 + z)
    NEXT_X = (NEXT[0], ((y + edge_next) % 2) * 4 + z)

    pos = {
        "o": j,
        "ou": y * 4 + z_up,
        "od": y * 4 + z_dn,
        "of": y * 4 + z_far,
        "x": other * 4 + z,
        "xu": other * 4 + z_up,
        "xd": other * 4 + z_dn,
        "xf": other * 4 + z_far,
    }

    def rows(b, chunk):
        return pl.ds(pl.multiple_of(BASE[b] + pos[chunk] * RB[b], 16), RB[b])

    def batch(b):
        return pl.ds(BASE[b], M[b])

    numbers = {}

    def number(key):
        return numbers.setdefault(key, len(numbers))

    def remote(key, src, dst, device):
        i = number(key)
        return pltpu.make_async_remote_copy(
            src_ref=src,
            dst_ref=dst,
            send_sem=send.at[i],
            recv_sem=recv.at[i],
            device_id=device,
            device_id_type=MESH,
        )

    sent = []

    def start(key, src, dst, device):
        copy = remote(key, src, dst, device)
        copy.start()
        sent.append((key, copy))

    def arrive(key, dst, device):
        remote(key, dst, dst, device).wait_recv()

    locals_ = {}

    def fetch(key, src, dst):
        copy = pltpu.make_async_copy(src, dst, local.at[len(locals_)])
        locals_[key] = copy
        copy.start()

    done = set()

    def need(key):
        if key not in done:
            done.add(key)
            locals_[key].wait()

    barrier = pltpu.get_barrier_semaphore()
    for step in range(1, N):
        pl.semaphore_signal(barrier, inc=1, device_id=(member, (j + step) % N), device_id_type=MESH)
    for to in (NEXT[0], PREV[0]):
        for at in (y, other):
            pl.semaphore_signal(barrier, inc=1, device_id=(to, at * 4 + z), device_id_type=MESH)
    for b in range(NB):
        fetch(("t", b), tokens.at[0, pl.ds(FIRST[b], RB[b])], tok.at[rows(b, "o")])
    left, right = pl.ds(0, FB), pl.ds(FB, FB)
    fetch("sg", stale_gate.at[0], sgu.at[:, left])
    fetch("su", stale_up.at[0], sgu.at[:, right])
    fetch("sd", stale_down.at[0], sd)
    fetch("wg", gate_w.at[0], wgu.at[:, left])
    fetch("wu", up_w.at[0], wgu.at[:, right])
    fetch("wd", down_w.at[0], wd)
    fetch("ups", upstream.at[0], ups)
    acc[...] = jnp.zeros_like(acc)
    pl.semaphore_wait(barrier, N + 3)

    mirror = {"ou": "od", "od": "ou", "xu": "xd", "xd": "xu"}

    def side(b, chunk):
        return mirror.get(chunk, chunk) if b % 2 else chunk

    def ways(b):
        return (DN, UP) if b % 2 else (UP, DN)

    def onward(b, chunk):
        chunk = side(b, chunk)
        if chunk[0] == "o":
            start(("n", b, chunk), tok.at[rows(b, chunk)], tok_next.at[rows(b, chunk)], PREV)
        else:
            at = ((other + edge_prev) % 2) * 4 + pos[chunk] % 4
            r = pl.ds(pl.multiple_of(BASE[b] + at * RB[b], 16), RB[b])
            start(("n", b, chunk), tok.at[r], tok_next.at[r], PREV_X)

    def gather(name, ref, then, crossings):
        def move(b, chunk, way, device):
            r = rows(b, side(b, chunk))
            start((name, b, chunk, way), ref.at[r], ref.at[r], device)

        def got(b, chunk, sent_as, way):
            arrive((name, b, sent_as, way), ref.at[rows(b, side(b, chunk))], UP)

        def e1(b):
            up, dn = ways(b)
            if name == "g":
                move(b, "o", "a", ACROSS)
            elif b == 0:
                for each in range(NB):
                    need(("t", each))
                    move(each, "o", "a", ACROSS)
                    if each == 0:
                        move(b, "o", "u", up)
                        move(b, "o", "d", dn)
                then(b, "o")
                return
            move(b, "o", "u", up)
            move(b, "o", "d", dn)

        def e2(b):
            got(b, "od", "o", "u")
            if crossings[b] == 2:
                move(b, "od", "a", ACROSS)
            move(b, "od", "u", ways(b)[0])
            then(b, "od")

        def e3(b):
            got(b, "x", "o", "a")
            move(b, "x", "d", ways(b)[1])
            if crossings[b] == 1:
                move(b, "x", "u", ways(b)[0])
            then(b, "x")

        def e4(b):
            if crossings[b] == 2:
                got(b, "xd", "od", "a")
                move(b, "xd", "u", ways(b)[0])
            else:
                got(b, "xd", "x", "u")
            then(b, "xd")

        def e5(b):
            got(b, "ou", "o", "d")
            then(b, "ou")

        def e6(b):
            got(b, "xu", "x", "d")
            if crossings[b] == 1:
                move(b, "xu", "d", ways(b)[1])
            then(b, "xu")

        def e7(b):
            got(b, "of", "od", "u")
            if crossings[b] == 2:
                got(b, "xf", "xd", "u")
            else:
                got(b, "xf", "xu", "d")
            then(b, "of")
            then(b, "xf")

        return e1, e2, e3, e4, e5, e6, e7

    def scatter(name, ref, land, crossings):
        def slot(b, k):
            return land.at[pl.ds(7 * FIRST[b] + k * RB[b], RB[b])]

        def push(b, chunk, k, device):
            start((name, b, k), ref.at[rows(b, side(b, chunk))], slot(b, k), device)

        def merge(b, chunk, slots, k, device):
            for each in slots:
                arrive((name, b, each), slot(b, each), UP)
            total = ref[rows(b, side(b, chunk)), :].astype(F32)
            for each in slots:
                total = total + slot(b, each)[...].astype(F32)
            at = slot(b, slots[0])
            at[...] = total.astype(BF16)
            start((name, b, k), at, slot(b, k), device)

        def last(b):
            return (3, 5, 6) if crossings[b] == 2 else (2, 5, 6)

        def f1(b):
            up, dn = ways(b)
            if crossings[b] == 2:
                push(b, "xf", 0, dn)
                push(b, "xu", 2, up)
                push(b, "of", 1, dn)
                push(b, "ou", 3, up)
            else:
                push(b, "xf", 0, up)
                push(b, "xd", 3, dn)
                push(b, "of", 1, dn)
                push(b, "ou", 2, up)

        def f2(b):
            if crossings[b] == 2:
                merge(b, "xd", (0,), 4, ACROSS)
            else:
                merge(b, "xu", (0,), 4, ways(b)[0])

        def f2b(b):
            if crossings[b] == 2:
                merge(b, "x", (2,), 5, ACROSS)
            else:
                merge(b, "od", (1,), 5, ways(b)[1])

        def f3(b):
            if crossings[b] == 2:
                merge(b, "od", (1, 4), 6, ways(b)[1])
            else:
                merge(b, "x", (3, 4), 6, ACROSS)

        def f4(b):
            for k in last(b):
                arrive((name, b, k), slot(b, k), UP)

        def result(b, first, size):
            at = pl.multiple_of(BASE[b] + j * RB[b] + first, 16)
            total = ref[pl.ds(at, size), :].astype(F32)
            for k in last(b):
                total = total + land[pl.ds(7 * FIRST[b] + k * RB[b] + first, size), :].astype(F32)
            return total

        return f1, f2, f2b, f3, f4, result

    ea = gather("a", tok, onward, CROSS["a"])
    eg = gather("g", go, lambda b, chunk: None, CROSS["g"])
    ra = scatter("r", gap, rs1, CROSS["r"])
    rg = scatter("s", peer, rs2, CROSS["s"])

    gain_row = gain[...].astype(F32)
    stale_row = stale_gain[...].astype(F32)

    def normalize(src, dst, at_dst, b, factor, keep):
        def body(at):
            values = src[pl.ds(pl.multiple_of(BASE[b] + at, 16), 16), :].astype(F32)
            scale = lax.rsqrt(jnp.mean(values * values, axis=-1, keepdims=True) + EPS)
            dst[pl.ds(pl.multiple_of(at_dst + at, 16), 16), :] = (values * scale * factor).astype(BF16)
            if keep:
                inv[pl.ds(pl.multiple_of(BASE[b] + at, 16), 16), :] = scale

        blocks(M[b], 16, body)

    def activate(b, ref, base, dst, at_dst):
        def body(at):
            r = pl.ds(pl.multiple_of(base + at, 16), 16)
            g, u = ref[r, left], ref[r, right]
            dst[pl.ds(pl.multiple_of(at_dst + at, 16), 16), :] = (g * jax.nn.sigmoid(g) * u).astype(BF16)

        blocks(M[b], 16, body)

    def p1(b):
        for chunk in pos:
            arrive(("n", b, chunk), tok_next.at[rows(b, chunk)], PREV)
        normalize(tok_next, xs, 0, b, stale_row, False)

    def p2(b):
        need("sg")
        need("su")
        own = pl.ds(0, M[b])
        gut[own, :] = dot_nn(xs[own, :], sgu[...])
        activate(b, gut, 0, hid_s, 0)

    def p4(b):
        need("sd")
        peer[batch(b), :] = dot_nn(hid_s[pl.ds(0, M[b]), :], sd[...]).astype(BF16)
        for half, device in ((0, NEXT), (1, NEXT_X)):
            r = pl.ds(BASE[b] + half * (M[b] // 2), M[b] // 2)
            start(("p", b, half), peer.at[r], gap.at[r], device)

    def o1(b):
        normalize(tok, x, BASE[b], b, gain_row, True)

    def o2(b):
        need("wg")
        need("wu")
        guv[batch(b), :] = dot_nn(x[batch(b), :], wgu[...])
        activate(b, guv, BASE[b], hid, BASE[b])

    def f0(b):
        need("wd")
        for half in range(2):
            arrive(("p", b, half), gap.at[pl.ds(BASE[b] + half * (M[b] // 2), M[b] // 2)], PREV)
        own = dot_nn(hid[batch(b), :], wd[...])
        gap[batch(b), :] = (own - gap[batch(b), :].astype(F32)).astype(BF16)
        ra[0](b)

    def f4(b):
        need("ups")
        ra[4](b)
        for first in range(0, RB[b], 16):
            total = ra[5](b, first, 16)
            mine = ups[pl.ds(FIRST[b] + first, 16), :].astype(F32) + AGREE * total
            go[pl.ds(pl.multiple_of(BASE[b] + j * RB[b] + first, 16), 16), :] = mine.astype(BF16)
        eg[0](b)

    def b1(b):
        gut[pl.ds(0, M[b]), left] = dot_nt(go[batch(b), :], wd[...])

        def body(at):
            r = pl.ds(pl.multiple_of(BASE[b] + at, 16), 16)
            g, u = guv[r, left], guv[r, right]
            s = jax.nn.sigmoid(g)
            gh = gut[pl.ds(at, 16), left]
            gp[r, left] = (gh * u * s * (1.0 + g * (1.0 - s))).astype(BF16)
            gp[r, right] = (gh * (g * s)).astype(BF16)

        blocks(M[b], 16, body)

    waited = set()

    def b2(b):
        for key, copy in sent:
            if key[:2] == ("p", b):
                copy.wait_send()
                waited.add(key)
        peer[batch(b), :] = dot_nt(gp[batch(b), :], wgu[...]).astype(BF16)
        rg[0](b)

    def b4(b):
        def body(at):
            r = pl.ds(pl.multiple_of(BASE[b] + at, 16), 16)
            part = peer[r, :].astype(F32) * (tok[r, :].astype(F32) * inv[r, :])
            acc[...] += part[:8] + part[8:]

        blocks(M[b], 16, body)

    def k1(b):
        acc_out[...] = jnp.sum(acc[...], axis=0, keepdims=True)
        for step in range(1, N):
            start(("k", step), acc_out, acc_in.at[step], (member, (j + step) % N))

    def k2(b):
        total = acc_out[...]
        for step in range(1, N):
            arrive(("k", step), acc_in.at[step], (member, (j + step) % N))
            total = total + acc_in[step]
        gain_buf[...] = total
        fetch("ok", gain_buf, out_gain)

    def f4g(b):
        rg[4](b)
        for first in range(0, RB[b], 16):
            grad_in = rg[5](b, first, 16)
            r = pl.ds(pl.multiple_of(BASE[b] + j * RB[b] + first, 16), 16)
            scale = inv[r, :]
            normed = tok[r, :].astype(F32) * scale
            grad_normed = grad_in * gain_row
            mean = jnp.mean(grad_normed * normed, axis=-1, keepdims=True)
            if b < NB - 1:
                part = grad_in * normed
                acc[...] += part[:8] + part[8:]
            outt[pl.ds(FIRST[b] + first, 16), :] = (
                go[r, :].astype(F32) + scale * (grad_normed - normed * mean)
            ).astype(BF16)
        r = pl.ds(FIRST[b], RB[b])
        fetch(("ot", b), outt.at[r], out_tokens.at[0, r])

    def weight_down(i):
        r = pl.ds(i * 256, 256)
        sd[r, :] = dot_tn(hid[:, i * 256 : (i + 1) * 256], go[...]).astype(BF16)
        fetch(("d", i), sd.at[r], out_down.at[0, r])

    def weight_up(i):
        r = pl.ds(i * 256, 256)
        sgu[r, :] = dot_tn(x[:, i * 256 : (i + 1) * 256], gp[...]).astype(BF16)
        fetch(("g", i), sgu.at[r, left], out_gate.at[0, r])
        fetch(("u", i), sgu.at[r, right], out_up.at[0, r])

    def n1(b):
        onward(b, "o")

    tasks = {
        "N": n1,
        "P1": p1, "P2": p2, "P4": p4, "O1": o1, "O2": o2, "F0": f0, "F4": f4,
        "F2": ra[1], "F2b": ra[2], "F3": ra[3], "S2": rg[1], "S2b": rg[2], "S3": rg[3], "S4": f4g,
        "B1": b1, "B2": b2, "B4": b4, "K1": k1, "K2": k2, "WD": weight_down, "WU": weight_up,
    }
    for i in range(7):
        tasks["E%d" % (i + 1)] = ea[i]
        tasks["G%d" % (i + 1)] = eg[i]
    for name, index in ORDER:
        tasks[name](index)

    for key, copy in sent:
        if key not in waited:
            copy.wait_send()
    for key in locals_:
        need(key)


def hand_over(*refs):
    sources, results, holds, sems = refs[:5], refs[5:10], refs[10:15], refs[15]
    steps = []
    for i, (src, hold, dst) in enumerate(zip(sources, holds, results)):
        whole = src.shape[1]
        parts = 4 if 0 < i < 4 else 1
        for part in range(parts):
            r = pl.ds(part * (whole // parts), whole // parts)
            steps.append((
                pltpu.make_async_copy(src.at[:, r], hold.at[:, r], sems.at[0, i, part]),
                pltpu.make_async_copy(hold.at[:, r], dst.at[:, r], sems.at[1, i, part]),
            ))
    for first, _ in steps:
        first.start()
    for first, second in steps:
        first.wait()
        second.start()
    for _, second in steps:
        second.wait()


def shards(
    tokens, upstream, gate_weight, up_weight, down_weight, norm_gain,
    stale_gate, stale_up, stale_down, stale_gain,
):
    hbm = pl.BlockSpec(memory_space=pl.ANY)
    vmem = pl.BlockSpec(memory_space=pltpu.VMEM)
    total = N * ROWS
    wide = pltpu.VMEM((total, D), BF16)
    half = pltpu.VMEM((total, FB), BF16)
    square = pltpu.VMEM((D, D), BF16)
    flat = pltpu.VMEM((FB, D), BF16)
    land = pltpu.VMEM((7 * ROWS, D), BF16)
    results = (
        jax.ShapeDtypeStruct((1, ROWS, D), BF16),
        jax.ShapeDtypeStruct((1, D, FB), BF16),
        jax.ShapeDtypeStruct((1, D, FB), BF16),
        jax.ShapeDtypeStruct((1, FB, D), BF16),
        jax.ShapeDtypeStruct((1, D), F32),
    )
    parts = pl.pallas_call(
        kernel,
        out_shape=results,
        in_specs=[hbm, hbm, hbm, hbm, hbm, vmem, hbm, hbm, hbm, vmem],
        out_specs=(hbm,) * 5,
        scratch_shapes=[
            square, flat, square, flat,
            pltpu.VMEM((ROWS, D), BF16),
            wide, wide, wide,
            pltpu.VMEM((max(M), D), BF16),
            pltpu.VMEM((total, 1), F32),
            pltpu.VMEM((total, D), F32), pltpu.VMEM((max(M), D), F32), half,
            pltpu.VMEM((max(M), FB), BF16),
            wide, wide, land, land, wide, wide,
            pltpu.VMEM((ROWS, D), BF16),
            pltpu.VMEM((8, D), F32),
            pltpu.VMEM((1, D), F32),
            pltpu.VMEM((N, 1, D), F32),
            pltpu.VMEM((1, D), F32),
            pltpu.SemaphoreType.DMA((NB * 38 + 8,)),
            pltpu.SemaphoreType.DMA((NB * 38 + 8,)),
            pltpu.SemaphoreType.DMA((2 * NB + 7 + 16,)),
        ],
        compiler_params=pltpu.CompilerParams(
            collective_id=0, has_side_effects=True, vmem_limit_bytes=62 * 2**20
        ),
        name="layer",
    )(
        tokens, upstream, gate_weight, up_weight, down_weight, norm_gain,
        stale_gate, stale_up, stale_down, stale_gain,
    )
    return pl.pallas_call(
        hand_over,
        out_shape=results,
        in_specs=[hbm] * 5,
        out_specs=(hbm,) * 5,
        scratch_shapes=[pltpu.VMEM(r.shape, r.dtype) for r in results]
        + [pltpu.SemaphoreType.DMA((2, 5, 4))],
        compiler_params=pltpu.CompilerParams(vmem_limit_bytes=62 * 2**20),
        name="hand_over",
    )(*parts)


def solution(mesh):
    in_specs = (
        P("member", "fsdp", None),
        P("member", "fsdp", None),
        P("member", None, "fsdp"),
        P("member", None, "fsdp"),
        P("member", "fsdp", None),
        P("member", None),
        P("member", None, "fsdp"),
        P("member", None, "fsdp"),
        P("member", "fsdp", None),
        P("member", None),
    )
    out_specs = (
        P("member", "fsdp", None),
        P("member", None, "fsdp"),
        P("member", None, "fsdp"),
        P("member", "fsdp", None),
        P("member", None),
    )
    return jax.shard_map(shards, mesh=mesh, in_specs=in_specs, out_specs=out_specs, check_vma=False)
```
